256 devices in a mesh: blk: 32 (over z, x_hi, core), outer: 8 (over x_lo, y).
Axes of the slice: x: 4 (x_hi: 2, x_lo: 2; x = x_hi * 2 + x_lo), y: 4, z: 8, core: 2. Of those that a mesh axis runs over, the one named last changes fastest.
Arguments:
- queries: float32 [16384, 1024], P('blk')
- passages: float32 [16384, 1024], P(('outer', 'blk'))
- positive_id: int32 [16384], P('blk'), may hold values from 0 to 16383, as said below
Outputs:
- question_derivative_matrix: float32 [16384, 1024], P('blk')
- grad_passages: float32 [16384, 1024], P(('outer', 'blk'))
- loss: float32 [], replicated
The draws below stay inside these ranges and needn't reach their ends.
Inputs may be any that keep to these rules, and one draw needn't show every extreme that they name: `positive_id`: a permutation: every passage is the positive of exactly one query.
All inputs are finite; a program needn't handle non-finite values.
Results may differ from the reference program's by a relative error of at most 0.007.
Values may be sent and summed in bfloat16 or wider, within the bound.
A program may use at most 64 MiB of HBM per device.

```python
import math
import jax
import jax.numpy as jnp
from jax import lax

D = 1024
PAIRS = 16384


def pairing(key):
    return jax.random.permutation(jax.random.fold_in(key, 11), PAIRS).astype(jnp.int32)


def passage_directions(key, turn_ramp, spread_lo):
    random_part = jax.random.normal(jax.random.fold_in(key, 12), (PAIRS, D), jnp.float32)
    spread = jnp.exp(jax.random.uniform(jax.random.fold_in(key, 14), (PAIRS, 1), jnp.float32, math.log(spread_lo), 1e-06))
    position = jnp.arange(PAIRS, dtype=jnp.float32)[:, None] / PAIRS
    turned = jax.random.uniform(jax.random.fold_in(key, 15), (PAIRS, 1), jnp.float32) < turn_ramp * position
    regular = spread * random_part
    tilted = 0.1 * random_part
    return jnp.where(turned, tilted, regular)


def row_scales(key):
    factor = jnp.exp(jax.random.uniform(key, (PAIRS, 1), jnp.float32, 0.0, math.log(10.0)))
    return factor / math.sqrt(D)


def draw_positive_id(key, part):
    return pairing(key)


def draw_passages(key, part):
    directions = passage_directions(key, 0.0, 1.0)
    key = jax.random.fold_in(key, 3)
    return directions * row_scales(jax.random.fold_in(key, 1))


def draw_queries(key, part):
    pairing_ids = pairing(key)
    directions = passage_directions(key, 0.0, 1.0)
    key = jax.random.fold_in(key, 4)
    jitter = jax.random.normal(jax.random.fold_in(key, 1), (PAIRS, D), jnp.float32)
    partner = directions[pairing_ids]
    blended = 0.17 * partner + jitter
    return blended * row_scales(jax.random.fold_in(key, 6))


def setup_inputs(seed: int = 0) -> dict:
    streams_of = jax.random.split(jax.random.key(seed), 4)
    return {
        "queries": draw_queries(jax.random.fold_in(streams_of[3], 71), 0),
        "passages": draw_passages(jax.random.fold_in(streams_of[3], 71), 0),
        "positive_id": draw_positive_id(jax.random.fold_in(streams_of[3], 71), 0),
    }


inverse_sharpness = 125.0
norm_epsilon = 1e-06

def normalize(values):
    squares = lax.optimization_barrier(jnp.sum(values * values, axis=1, keepdims=True))
    inverse = lax.rsqrt(squares + norm_epsilon)
    return (values * inverse, inverse)

def chain_through_rescaling(unit, inverse, upstream):
    along = lax.optimization_barrier(jnp.sum(unit * upstream, axis=1, keepdims=True))
    return inverse * (upstream - unit * along)

def positive_mask(positive_id, column_start, count):
    columns = column_start + lax.iota(jnp.int32, count)
    return (positive_id[None, :] == columns[:, None]).astype(jnp.float32)

def pair_weights(cosine_logit_matrix, row_lse, col_lse, mask):
    mixed = 0.5 * (jnp.exp(cosine_logit_matrix - row_lse[None, :]) + jnp.exp(cosine_logit_matrix - col_lse[:, None])) - mask
    return mixed.astype(jnp.bfloat16)

def reference(queries, passages, positive_id):
    question_direction_entry, question_inverse_length = normalize(queries)
    passage_unit, passage_inverse = normalize(passages)
    question_objective_term = question_direction_entry.astype(jnp.bfloat16)
    passage_half = passage_unit.astype(jnp.bfloat16)
    width = math.gcd(PAIRS, 512)
    count = PAIRS // width
    offsets = jnp.arange(count, dtype=jnp.int32) * width

    def first_block(carried, offset):
        row_top, row_total, positive_sum = carried
        tile_span = lax.dynamic_slice_in_dim(passage_half, offset, width, 0)
        cosine_logit_matrix = inverse_sharpness * jnp.dot(tile_span, question_objective_term.T, preferred_element_type=jnp.float32)
        mask = positive_mask(positive_id, offset, width)
        col_top = lax.optimization_barrier(jnp.max(cosine_logit_matrix, axis=1))
        col_lse = col_top + jnp.log(lax.optimization_barrier(jnp.sum(jnp.exp(cosine_logit_matrix - col_top[:, None]), axis=1)))
        new_top = jnp.maximum(row_top, lax.optimization_barrier(jnp.max(cosine_logit_matrix, axis=0)))
        row_total = row_total * jnp.exp(row_top - new_top) + lax.optimization_barrier(jnp.sum(jnp.exp(cosine_logit_matrix - new_top[None, :]), axis=0))
        positive_sum = positive_sum + jnp.sum(cosine_logit_matrix * mask)
        return ((new_top, row_total, positive_sum), col_lse)
    start = (jnp.full((PAIRS,), -jnp.inf, jnp.float32), jnp.zeros((PAIRS,), jnp.float32), jnp.zeros((), jnp.float32))
    (row_top, row_total, positive_sum), col_lse = lax.scan(first_block, start, offsets)
    row_lse = row_top + jnp.log(row_total)
    col_lse = col_lse.reshape(PAIRS)
    loss = (jnp.sum(row_lse) + jnp.sum(col_lse) - 2.0 * positive_sum) / (2.0 * PAIRS)

    def second_block(question_derivative, offset):
        tile_span = lax.dynamic_slice_in_dim(passage_half, offset, width, 0)
        cosine_logit_matrix = inverse_sharpness * jnp.dot(tile_span, question_objective_term.T, preferred_element_type=jnp.float32)
        mask = positive_mask(positive_id, offset, width)
        block_lse = lax.dynamic_slice_in_dim(col_lse, offset, width, 0)
        probability_matrix = pair_weights(cosine_logit_matrix, row_lse, block_lse, mask)
        question_derivative = question_derivative + jnp.dot(probability_matrix.T, tile_span, preferred_element_type=jnp.float32)
        document_share = inverse_sharpness * jnp.dot(probability_matrix, question_objective_term, preferred_element_type=jnp.float32)
        return (question_derivative, document_share)
    question_derivative, passage_parts = lax.scan(second_block, jnp.zeros((PAIRS, D), jnp.float32), offsets)
    question_derivative_matrix = chain_through_rescaling(question_direction_entry, question_inverse_length, inverse_sharpness * question_derivative)
    grad_passages = chain_through_rescaling(passage_unit, passage_inverse, passage_parts.reshape(PAIRS, D))
    return (question_derivative_matrix, grad_passages, loss)
```

```python
import jax
import jax.numpy as jnp
from jax import lax
from jax.sharding import PartitionSpec as P

inverse_sharpness = 125.0
norm_epsilon = 1e-06


def normalize(values):
    squares = jnp.sum(values * values, axis=1, keepdims=True)
    inverse = lax.rsqrt(squares + norm_epsilon)
    return (values * inverse, inverse)


def chain_through_rescaling(unit, inverse, upstream):
    along = jnp.sum(unit * upstream, axis=1, keepdims=True)
    return inverse * (upstream - unit * along)


def per_device(queries, passages, positive_id):
    blk_count = lax.axis_size("blk")
    outer_count = lax.axis_size("outer")
    outer_index = lax.axis_index("outer")
    block_rows = passages.shape[0]
    super_cols = block_rows * blk_count
    column_base = outer_index * super_cols
    q_unit, q_inv = normalize(queries)
    p_unit, p_inv = normalize(passages)
    q_half = q_unit.astype(jnp.bfloat16)
    p_half = p_unit.astype(jnp.bfloat16)
    p_all = lax.all_gather(p_half, "blk", axis=0, tiled=True)
    scores = inverse_sharpness * jnp.einsum(
        "pd,qd->pq", p_all, q_half, preferred_element_type=jnp.float32
    )
    columns = column_base + lax.iota(jnp.int32, super_cols)
    mask = (positive_id[None, :] == columns[:, None]).astype(jnp.float32)
    col_top = jnp.max(scores, axis=1)
    col_total = jnp.sum(jnp.exp(scores - col_top[:, None]), axis=1)
    row_top = jnp.max(scores, axis=0)
    row_total = jnp.sum(jnp.exp(scores - row_top[None, :]), axis=0)
    positive = jnp.sum(scores * mask, axis=0)
    col_all = lax.all_gather(jnp.stack([col_top, col_total]), "blk")
    row_all = lax.all_gather(jnp.stack([row_top, row_total, positive]), "outer")
    col_max = jnp.max(col_all[:, 0], axis=0)
    col_lse = col_max + jnp.log(
        jnp.sum(col_all[:, 1] * jnp.exp(col_all[:, 0] - col_max[None]), axis=0)
    )
    row_max = jnp.max(row_all[:, 0], axis=0)
    row_lse = row_max + jnp.log(
        jnp.sum(row_all[:, 1] * jnp.exp(row_all[:, 0] - row_max[None]), axis=0)
    )
    positives = jnp.sum(row_all[:, 2])
    local = (jnp.sum(row_lse) - 2.0 * positives) / outer_count + jnp.sum(col_lse) / blk_count
    loss = lax.psum(local, ("blk", "outer")) / (2.0 * super_cols * outer_count)
    weights = (
        0.5 * (jnp.exp(scores - row_lse[None, :]) + jnp.exp(scores - col_lse[:, None])) - mask
    ).astype(jnp.bfloat16)
    p_part = inverse_sharpness * jnp.einsum(
        "pq,qd->pd", weights, q_half, preferred_element_type=jnp.float32
    )
    p_grad = lax.psum_scatter(p_part, "blk", scatter_dimension=0, tiled=True)
    q_part = inverse_sharpness * jnp.einsum(
        "pq,pd->qd", weights, p_all, preferred_element_type=jnp.float32
    )
    q_grad = lax.psum(q_part, "outer")
    return (
        chain_through_rescaling(q_unit, q_inv, q_grad),
        chain_through_rescaling(p_unit, p_inv, p_grad),
        loss,
    )


def solution(mesh):
    placed = (P("blk", None), P(("outer", "blk"), None), P("blk"))
    return jax.shard_map(
        per_device,
        mesh=mesh,
        in_specs=placed,
        out_specs=(P("blk", None), P(("outer", "blk"), None), P()),
        check_vma=False,
    )
```

```python
import jax
import jax.numpy as jnp
from jax import lax
from jax.experimental import pallas as pl
from jax.experimental.pallas import tpu as pltpu
from jax.sharding import PartitionSpec as P

MESH = pl.DeviceIdType.MESH
SHARP = 125.0
EPS = 1e-06
D = 1024
NQ = 512
NP = 64
NB = 32
NO = 8
NZ = 8
GROUP = 4 * NP
F32 = jnp.float32
BF16 = jnp.bfloat16
NT = (((1,), (1,)), ((), ()))
NN = (((1,), (0,)), ((), ()))
TN = (((0,), (0,)), ((), ()))


def dot(a, b, dims):
    return lax.dot_general(a, b, dims, preferred_element_type=F32)


def lse_of(parts, axis):
    top = jnp.max(parts, axis=axis, keepdims=True)
    return top + jnp.log(jnp.sum(jnp.exp(parts - top), axis=axis, keepdims=True))


def kernel(
    q_ref, p_ref, id_ref,
    qo_ref, po_ref, loss_ref,
    pall, qh, scores, weights, mine, pres, sib_out, sib_in, ring_out, ring_in,
    x_out, x_in, q_out, q_in, q_fin, q_own,
    row_part, pos_acc, col_part, col_sib, col_chip, col_all, row_all,
    sum_r, sum_r_sib, sum_r_chip, sum_r_all, sum_c_all,
    ag_ss, ag_rs, cs_ss, cs_rs, col_ss, col_rs, row_ss, row_rs,
    sib_ss, sib_rs, ring_ss, ring_rs, x_ss, x_rs, q_ss, q_rs, f_ss, f_rs,
    r1_ss, r1_rs, ra_ss, ra_rs, ca_ss, ca_rs,
):
    b = lax.axis_index("blk")
    o = lax.axis_index("outer")
    c = lax.rem(b, 2)
    xh = lax.rem(lax.div(b, 2), 2)
    z = lax.div(b, 4)
    chip = z * 2 + xh

    def blk_of(zz, xx, cc):
        return (zz * 2 + xx) * 2 + cc

    def wrap(dz):
        return lax.rem(z + dz + 16, NZ)

    def at(zz, xx, cc):
        return (blk_of(zz, xx, cc), o)

    sib = at(z, xh, 1 - c)
    x2 = at(z, 1 - xh, c)
    up = at(wrap(1), xh, c)
    down = at(wrap(-1), xh, c)

    def chip_peer(k):
        other = lax.rem(chip + k, 16)
        return other, (other * 2 + c, o)

    def outer_peer(k):
        other = lax.rem(o + k, NO)
        return other, (b, other)

    def copy(src, dst, ss, rs, dev):
        return pltpu.make_async_remote_copy(
            src_ref=src, dst_ref=dst, send_sem=ss, recv_sem=rs, device_id=dev, device_id_type=MESH
        )

    barrier = pltpu.get_barrier_semaphore()
    pl.semaphore_signal(barrier, inc=1, device_id=sib, device_id_type=MESH)

    def greet_chip(k, _):
        pl.semaphore_signal(barrier, inc=1, device_id=chip_peer(k)[1], device_id_type=MESH)
        return 0

    def greet_outer(k, _):
        pl.semaphore_signal(barrier, inc=1, device_id=outer_peer(k)[1], device_id_type=MESH)
        return 0

    lax.fori_loop(1, 16, greet_chip, 0)
    lax.fori_loop(1, NO, greet_outer, 0)

    def rows(i, n=NP):
        return pl.ds(pl.multiple_of(i * n, n), n)

    def shard(i):
        return pall.at[rows(i)]

    pv = p_ref[...]
    p_inv = lax.rsqrt(jnp.sum(pv * pv, axis=1, keepdims=True) + EPS)
    pall[rows(b), :] = (pv * p_inv).astype(BF16)
    pl.semaphore_wait(barrier, 23)

    def ag_copy(i, k, dev):
        return copy(shard(i), shard(i), ag_ss.at[k], ag_rs.at[i], dev)

    def ag_send(i, k, *devs):
        for n, dev in enumerate(devs):
            ag_copy(i, k + n, dev).start()

    def ag_wait(i):
        ag_copy(i, 0, sib).wait_recv()

    ag_send(b, 0, up, down, x2, sib)

    def norm_q(i, _):
        v = q_ref[rows(i), :]
        inv = lax.rsqrt(jnp.sum(v * v, axis=1, keepdims=True) + EPS)
        qh[rows(i), :] = (v * inv).astype(BF16)
        return 0

    lax.fori_loop(0, NQ // NP, norm_q, 0)
    pos_acc[...] = jnp.zeros_like(pos_acc)

    def own(dz, xrel):
        return blk_of(wrap(dz), xh if xrel == 0 else 1 - xh, c)

    def got(dz, xrel, k, *devs):
        i = own(dz, xrel)
        ag_wait(i)
        ag_send(i, k, *devs)

    def from_sib(dz):
        ag_wait(blk_of(wrap(dz), 0, 1 - c))
        ag_wait(blk_of(wrap(dz), 1, 1 - c))

    sign = 2 * xh - 1

    def far(xrel, k):
        s = sign if xrel == 0 else -sign
        i = blk_of(wrap(3 * s), xh if xrel == 0 else 1 - xh, c)
        ag_send(i, k, at(wrap(-s), xh, c))

    def gather_turn(t):
        if t == 0:
            got(0, 1, 4, sib)
            got(-1, 0, 5, up, x2, sib)
            got(1, 0, 8, down, x2, sib)
            from_sib(0)
        if t == 1:
            got(-1, 1, 11, sib)
            got(1, 1, 12, sib)
            got(-2, 0, 13, up, x2, sib)
            got(2, 0, 16, down, x2, sib)
            from_sib(-1)
        if t == 2:
            from_sib(1)
        if t == 3:
            got(-2, 1, 19, up, sib)
            got(2, 1, 21, down, sib)
            got(-3, 0, 23, sib)
            got(3, 0, 24, sib)
            far(0, 25)
            from_sib(-2)
        if t == 4:
            from_sib(2)
        if t == 5:
            got(-3, 1, 26, sib)
            got(3, 1, 27, sib)
            far(1, 28)
            from_sib(-3)
        if t == 6:
            got(4, 0, 29, sib)
            got(4, 1, 30, sib)
            from_sib(3)
        if t == 7:
            from_sib(4)

    base = o * (NB * NP)

    def mask_of(zz):
        cols = base + zz * GROUP + lax.broadcasted_iota(jnp.int32, (GROUP, NQ), 0)
        return cols == id_ref[...]

    def first(t, _):
        for k in range(8):
            pl.when(t == k)(lambda k=k: gather_turn(k))
        far_by = lax.div(t + 1, 2)
        zz = wrap(jnp.where(lax.rem(t, 2) == 1, -far_by, far_by))
        pg = pall[rows(zz, GROUP), :]
        s = SHARP * dot(pg, qh[...], NT)
        scores[rows(zz, GROUP), :] = s
        row_part[pl.ds(t, 1), :] = lse_of(s, 0)
        pos_acc[...] += jnp.sum(jnp.where(mask_of(zz), s, 0.0), axis=0, keepdims=True)
        st = SHARP * dot(qh[...], pg, NT)
        col_part[pl.ds(zz, 1), :] = lse_of(st, 0)
        return 0

    lax.fori_loop(0, 8, first, 0)

    sib_col = copy(col_part, col_sib, cs_ss.at[0], cs_rs.at[0], sib)
    sib_col.start()
    row_lse_part = lse_of(row_part[...], 0)
    pos_part = pos_acc[...]
    for k in range(4):
        row_all[o, k : k + 1, :] = row_lse_part[:, 128 * k : 128 * k + 128]
        row_all[o, 4 + k : 5 + k, :] = pos_part[:, 128 * k : 128 * k + 128]

    def row_copy(k):
        other, dev = outer_peer(k)
        send = copy(row_all.at[o], row_all.at[o], row_ss.at[k], row_rs.at[o], dev)
        recv = copy(row_all.at[o], row_all.at[other], row_ss.at[k], row_rs.at[other], dev)
        return send, recv

    def row_start(k, _):
        row_copy(k)[0].start()
        return 0

    lax.fori_loop(1, NO, row_start, 0)
    sib_col.wait_recv()
    a0, a1 = col_part[...], col_sib[...]
    top = jnp.maximum(a0, a1)
    col_all[chip] = top + jnp.log(jnp.exp(a0 - top) + jnp.exp(a1 - top))

    def col_copy(k):
        other, dev = chip_peer(k)
        send = copy(col_all.at[chip], col_all.at[chip], col_ss.at[k], col_rs.at[chip], dev)
        recv = copy(col_all.at[chip], col_all.at[other], col_ss.at[k], col_rs.at[other], dev)
        return send, recv

    def col_start(k, _):
        col_copy(k)[0].start()
        return 0

    lax.fori_loop(1, 16, col_start, 0)

    def row_wait(k, _):
        row_copy(k)[1].wait_recv()
        return 0

    lax.fori_loop(1, NO, row_wait, 0)
    rall = row_all[...]
    row_lse4 = lse_of(rall[:, 0:4, :], 0)[0]
    pos4 = jnp.sum(rall[:, 4:8, :], axis=0)
    row_lse = jnp.concatenate([row_lse4[k : k + 1, :] for k in range(4)], axis=1)
    sum_r[...] = jnp.broadcast_to(jnp.sum(row_lse4 - 2.0 * pos4, keepdims=True), (8, 128))
    sib_r = copy(sum_r, sum_r_sib, r1_ss.at[0], r1_rs.at[0], sib)
    sib_r.start()

    def col_wait(k, _):
        col_copy(k)[1].wait_recv()
        return 0

    lax.fori_loop(1, 16, col_wait, 0)
    col_lse = lse_of(col_all[...], 0)[0]
    col_chip[...] = col_lse
    sum_c_all[o] = jnp.broadcast_to(jnp.sum(col_lse, keepdims=True), (8, 128))

    def c_copy(k):
        other, dev = outer_peer(k)
        send = copy(sum_c_all.at[o], sum_c_all.at[o], ca_ss.at[k], ca_rs.at[o], dev)
        recv = copy(sum_c_all.at[o], sum_c_all.at[other], ca_ss.at[k], ca_rs.at[other], dev)
        return send, recv

    def sib_copy(i):
        return copy(sib_out.at[i], sib_in.at[i], sib_ss.at[i], sib_rs.at[i], sib)

    def joined(dz, xx):
        i = wrap(dz) * 2 + xx
        sib_copy(i).wait_recv()
        mine[i] = mine[i] + sib_in[i].astype(F32)

    def slot(way, d, xx):
        return way * 8 + (d - 1) * 2 + xx

    def ring_copy(way, d, xx):
        i = slot(way, d, xx)
        return copy(ring_out.at[i], ring_in.at[i], ring_ss.at[i], ring_rs.at[i], up if way == 0 else down)

    def ring_send(way, d, xx, carry):
        i = wrap(d if way == 0 else -d) * 2 + xx
        value = mine[i]
        if carry:
            ring_copy(way, d + 1, xx).wait_recv()
            value = value + ring_in[slot(way, d + 1, xx)].astype(F32)
        ring_out[slot(way, d, xx)] = value.astype(BF16)
        ring_copy(way, d, xx).start()

    def scatter_turn(t):
        if t == 1:
            joined(4, 0)
            joined(4, 1)
            ring_send(0, 4, 0, False)
            ring_send(1, 4, 1, False)
        if t == 3:
            joined(3, 1)
            joined(-3, 0)
            ring_send(0, 3, 1, False)
            ring_send(1, 3, 0, False)
            joined(3, 0)
            joined(-3, 1)
        if t == 5:
            for xx in range(2):
                joined(2, xx)
                joined(-2, xx)
        if t == 7:
            for xx in range(2):
                joined(1, xx)
                joined(-1, xx)

    def second(t, _):
        far_by = 4 - lax.div(t + 1, 2)
        zz = wrap(jnp.where(lax.rem(t, 2) == 1, far_by, -far_by))
        s = scores[rows(zz, GROUP), :]
        cl = jnp.broadcast_to(col_chip[pl.ds(zz, 1), :], (8, GROUP)).T[:, 0:1]
        w = 0.5 * (jnp.exp(s - row_lse) + jnp.exp(s - cl)) - jnp.where(mask_of(zz), 1.0, 0.0)
        w = w.astype(BF16)
        weights[rows(zz, GROUP), :] = w
        pres[...] = SHARP * dot(w, qh[...], NN)
        for xx in range(2):
            i = zz * 2 + xx
            sib_out[i] = pres[rows(xx * 2 + 1 - c), :].astype(BF16)
            sib_copy(i).start()
            mine[i] = pres[rows(xx * 2 + c), :]
        for k in (1, 3, 5, 7):
            pl.when(t == k)(lambda k=k: scatter_turn(k))
        return 0

    lax.fori_loop(0, 8, second, 0)

    def q_copy(other):
        dev = (b, other)
        send = copy(q_out.at[other], q_in.at[o], q_ss.at[other], q_rs.at[o], dev)
        recv = copy(q_out.at[other], q_in.at[other], q_ss.at[other], q_rs.at[other], dev)
        return send, recv

    def q_chunk(k, _):
        k = lax.rem(k + lax.div(o, 2), 4)
        w = weights[:, pl.ds(pl.multiple_of(k * 128, 128), 128)]
        g = dot(w, pall[...], TN)
        for h in range(2):
            other = 2 * k + h
            part = g[h * NP : (h + 1) * NP, :]

            @pl.when(other == o)
            def _():
                q_own[...] = part

            @pl.when(other != o)
            def _():
                q_out[other] = part.astype(BF16)
                q_copy(other)[0].start()

        return 0

    lax.fori_loop(0, 4, q_chunk, 0)

    def c_start(k, _):
        c_copy(k)[0].start()
        return 0

    lax.fori_loop(1, NO, c_start, 0)

    ring_send(0, 3, 0, True)
    ring_send(1, 3, 1, True)
    ring_send(0, 2, 1, True)
    ring_send(1, 2, 0, True)
    sib_r.wait_recv()
    sum_r_all[chip] = sum_r[...] + sum_r_sib[...]

    def r_copy(k):
        other, dev = chip_peer(k)
        send = copy(sum_r_all.at[chip], sum_r_all.at[chip], ra_ss.at[k], ra_rs.at[chip], dev)
        recv = copy(sum_r_all.at[chip], sum_r_all.at[other], ra_ss.at[k], ra_rs.at[other], dev)
        return send, recv

    def r_start(k, _):
        r_copy(k)[0].start()
        return 0

    lax.fori_loop(1, 16, r_start, 0)
    ring_send(0, 2, 0, True)
    ring_send(1, 2, 1, True)
    ring_send(0, 1, 1, True)
    ring_send(1, 1, 0, True)

    def q_add(k, _):
        other, _dev = outer_peer(k)
        q_copy(other)[1].wait_recv()
        q_own[...] += q_in[other].astype(F32)
        return 0

    lax.fori_loop(1, NO, q_add, 0)
    qv = q_ref[rows(o), :]
    q_inv = lax.rsqrt(jnp.sum(qv * qv, axis=1, keepdims=True) + EPS)
    qu = qv * q_inv
    qg = SHARP * q_own[...]
    q_fin[o] = (q_inv * (qg - qu * jnp.sum(qu * qg, axis=1, keepdims=True))).astype(BF16)

    def f_copy(k):
        other, dev = outer_peer(k)
        send = copy(q_fin.at[o], q_fin.at[o], f_ss.at[k], f_rs.at[o], dev)
        recv = copy(q_fin.at[o], q_fin.at[other], f_ss.at[k], f_rs.at[other], dev)
        return send, recv

    def f_start(k, _):
        f_copy(k)[0].start()
        return 0

    lax.fori_loop(1, NO, f_start, 0)

    ring_send(0, 1, 0, True)
    ring_send(1, 1, 1, True)

    def total(xx):
        i = z * 2 + xx
        for way in range(2):
            copy(
                ring_out.at[slot(way, 1, xx)], ring_in.at[slot(way, 1, xx)],
                ring_ss.at[slot(way, 1, xx)], ring_rs.at[slot(way, 1, xx)], up,
            ).wait_recv()
        return (
            mine[i]
            + ring_in[slot(0, 1, xx)].astype(F32)
            + ring_in[slot(1, 1, xx)].astype(F32)
        )

    joined(0, 0)
    joined(0, 1)
    x_out[...] = total(1 - xh).astype(BF16)
    x_copy = copy(x_out, x_in, x_ss.at[0], x_rs.at[0], x2)
    x_copy.start()
    pg_own = total(xh)

    def c_wait(k, _):
        c_copy(k)[1].wait_recv()
        return 0

    def r_wait(k, _):
        r_copy(k)[1].wait_recv()
        return 0

    lax.fori_loop(1, NO, c_wait, 0)
    lax.fori_loop(1, 16, r_wait, 0)
    loss_ref[...] = (jnp.sum(sum_r_all[...], axis=0) + jnp.sum(sum_c_all[...], axis=0)) / (
        2.0 * NB * NP * NO
    )

    qo_ref[rows(o), :] = q_fin[o].astype(F32)

    def f_wait(k, _):
        other, _dev = outer_peer(k)
        f_copy(k)[1].wait_recv()
        qo_ref[rows(other), :] = q_fin[other].astype(F32)
        return 0

    lax.fori_loop(1, NO, f_wait, 0)

    x_copy.wait_recv()
    pu = p_ref[...]
    p_inv2 = lax.rsqrt(jnp.sum(pu * pu, axis=1, keepdims=True) + EPS)
    pu = pu * p_inv2
    g = pg_own + x_in[...].astype(F32)
    po_ref[...] = p_inv2 * (g - pu * jnp.sum(pu * g, axis=1, keepdims=True))

    def ag_done(k, _):
        ag_copy(b, k, sib).wait_send()
        return 0

    lax.fori_loop(0, 31, ag_done, 0)
    sib_col.wait_send()
    sib_r.wait_send()
    x_copy.wait_send()

    def outer_done(k, _):
        row_copy(k)[0].wait_send()
        c_copy(k)[0].wait_send()
        f_copy(k)[0].wait_send()
        q_copy(outer_peer(k)[0])[0].wait_send()
        return 0

    lax.fori_loop(1, NO, outer_done, 0)

    def chip_done(k, _):
        col_copy(k)[0].wait_send()
        r_copy(k)[0].wait_send()
        return 0

    lax.fori_loop(1, 16, chip_done, 0)

    def sib_done(k, _):
        sib_copy(k).wait_send()
        return 0

    lax.fori_loop(0, 16, sib_done, 0)
    for way in range(2):
        for d in (1, 2, 3, 4):
            for xx in range(2):
                if d < 4 or xx == way:
                    ring_copy(way, d, xx).wait_send()


def per_device(queries, passages, positive_id):
    vmem = pl.BlockSpec(memory_space=pltpu.VMEM)
    dma = pltpu.SemaphoreType.DMA
    scratch = [
        pltpu.VMEM((NB * NP, D), BF16),
        pltpu.VMEM((NQ, D), BF16),
        pltpu.VMEM((NB * NP, NQ), F32),
        pltpu.VMEM((NB * NP, NQ), BF16),
        pltpu.VMEM((16, NP, D), F32),
        pltpu.VMEM((GROUP, D), F32),
        pltpu.VMEM((16, NP, D), BF16),
        pltpu.VMEM((16, NP, D), BF16),
        pltpu.VMEM((16, NP, D), BF16),
        pltpu.VMEM((16, NP, D), BF16),
        pltpu.VMEM((NP, D), BF16),
        pltpu.VMEM((NP, D), BF16),
        pltpu.VMEM((NO, NP, D), BF16),
        pltpu.VMEM((NO, NP, D), BF16),
        pltpu.VMEM((NO, NP, D), BF16),
        pltpu.VMEM((NP, D), F32),
        pltpu.VMEM((8, NQ), F32),
        pltpu.VMEM((1, NQ), F32),
        pltpu.VMEM((NZ, GROUP), F32),
        pltpu.VMEM((NZ, GROUP), F32),
        pltpu.VMEM((NZ, GROUP), F32),
        pltpu.VMEM((16, NZ, GROUP), F32),
        pltpu.VMEM((NO, 8, 128), F32),
        pltpu.VMEM((8, 128), F32),
        pltpu.VMEM((8, 128), F32),
        pltpu.VMEM((8, 128), F32),
        pltpu.VMEM((16, 8, 128), F32),
        pltpu.VMEM((NO, 8, 128), F32),
        dma((31,)), dma((NB,)),
        dma((1,)), dma((1,)),
        dma((16,)), dma((16,)),
        dma((NO,)), dma((NO,)),
        dma((16,)), dma((16,)),
        dma((16,)), dma((16,)),
        dma((1,)), dma((1,)),
        dma((NO,)), dma((NO,)),
        dma((NO,)), dma((NO,)),
        dma((1,)), dma((1,)),
        dma((16,)), dma((16,)),
        dma((NO,)), dma((NO,)),
    ]
    qd, pd, loss = pl.pallas_call(
        kernel,
        out_shape=(
            jax.ShapeDtypeStruct((NQ, D), F32),
            jax.ShapeDtypeStruct((NP, D), F32),
            jax.ShapeDtypeStruct((8, 128), F32),
        ),
        in_specs=[vmem, vmem, vmem],
        out_specs=(vmem, vmem, vmem),
        scratch_shapes=scratch,
        compiler_params=pltpu.CompilerParams(
            collective_id=0, has_side_effects=True, vmem_limit_bytes=56 * 2**20
        ),
    )(queries, passages, positive_id.reshape(1, NQ))
    return qd, pd, loss[0, 0]


def solution(mesh):
    placed = (P("blk", None), P(("outer", "blk"), None), P("blk"))
    return jax.shard_map(
        per_device,
        mesh=mesh,
        in_specs=placed,
        out_specs=(P("blk", None), P(("outer", "blk"), None), P()),
        check_vma=False,
    )
```

```python
import jax
import jax.numpy as jnp
from jax import lax
from jax.experimental import pallas as pl
from jax.experimental.pallas import tpu as pltpu
from jax.sharding import PartitionSpec as P

MESH = pl.DeviceIdType.MESH
SHARP = 125.0
EPS = 1e-06
LN2 = 0.6931471805599453
SHARP2 = SHARP / LN2
HALF = 32
CROSS = (0,)
D = 1024
NQ = 512
NP = 64
NB = 32
NO = 8
NZ = 8
GROUP = 4 * NP
F32 = jnp.float32
BF16 = jnp.bfloat16
NT = (((1,), (1,)), ((), ()))
NN = (((1,), (0,)), ((), ()))
TN = (((0,), (0,)), ((), ()))


def dot(a, b, dims):
    return lax.dot_general(a, b, dims, preferred_element_type=F32)


def lse_of(parts, axis):
    top = jnp.max(parts, axis=axis, keepdims=True)
    return top + jnp.log(jnp.sum(jnp.exp2(parts - top), axis=axis, keepdims=True)) * (1.0 / LN2)


def kernel(
    q_any, p_any, id_any,
    q_fin, po_ref, loss_ref,
    q_ref, p_ref, id_ref, in_sem,
    pall, qh, scores, weights, mine, pres, sib_out, sib_in, ring_out, ring_in,
    x_out, x_in, q_out, q_in, q_own,
    row_part, row_wide, pos_acc, col_part, col_sib, col_wide, col_all, row_all,
    sum_r, sum_r_sib, sum_r_all, sum_c_all,
    ag_ss, ag_rs, as_ss, cs_ss, cs_rs, col_ss, col_rs, row_ss, row_rs,
    sib_ss, sib_rs, ring_ss, ring_rs, x_ss, x_rs, q_ss, q_rs, f_ss, f_rs,
    r1_ss, r1_rs, ra_ss, ra_rs, ca_ss, ca_rs,
):
    b = lax.axis_index("blk")
    o = lax.axis_index("outer")
    c = lax.rem(b, 2)
    xh = lax.rem(lax.div(b, 2), 2)
    z = lax.div(b, 4)
    chip = z * 2 + xh

    def blk_of(zz, xx, cc):
        return (zz * 2 + xx) * 2 + cc

    def wrap(dz):
        return lax.rem(z + dz + 16, NZ)

    def at(zz, xx, cc):
        return (blk_of(zz, xx, cc), o)

    sib = at(z, xh, 1 - c)
    x2 = at(z, 1 - xh, c)
    up = at(wrap(1), xh, c)
    down = at(wrap(-1), xh, c)

    def chip_peer(k):
        other = lax.rem(chip + k, 16)
        return other, (other * 2 + c, o)

    def outer_peer(k):
        other = lax.rem(o + k, NO)
        return other, (b, other)

    def copy(src, dst, ss, rs, dev):
        return pltpu.make_async_remote_copy(
            src_ref=src, dst_ref=dst, send_sem=ss, recv_sem=rs, device_id=dev, device_id_type=MESH
        )

    p_load = pltpu.make_async_copy(p_any, p_ref, in_sem.at[0])
    q_load = pltpu.make_async_copy(q_any, q_ref, in_sem.at[1])
    id_load = pltpu.make_async_copy(id_any, id_ref, in_sem.at[2])
    p_load.start()
    barrier = pltpu.get_barrier_semaphore()
    for dev in (x2, up, down, sib):
        pl.semaphore_signal(barrier, inc=1, device_id=dev, device_id_type=MESH)

    def greet_outer(k, _):
        pl.semaphore_signal(barrier, inc=1, device_id=outer_peer(k)[1], device_id_type=MESH)
        return 0

    lax.fori_loop(1, NO, greet_outer, 0)
    q_load.start()
    id_load.start()

    def rows(i, n=NP):
        return pl.ds(pl.multiple_of(i * n, n), n)

    def shard(i):
        return pall.at[rows(i)]

    p_load.wait()
    pv = p_ref[...]
    p_inv = lax.rsqrt(jnp.sum(pv * pv, axis=1, keepdims=True) + EPS)
    pall[rows(b), :] = (pv * p_inv).astype(BF16)
    pl.semaphore_wait(barrier, 4 + NO - 1)

    def piece(i, h):
        return pall.at[pl.ds(pl.multiple_of(i * NP + h * HALF, HALF), HALF)]

    def ag_copy(i, h, k, dev):
        return copy(piece(i, h), piece(i, h), ag_ss.at[k], ag_rs.at[i * 2 + h], dev)

    def as_copy(i, k):
        return copy(shard(i), shard(i), as_ss.at[k], ag_rs.at[i * 2], sib)

    sent = [0, 0]

    def pass_on(i, h, *devs):
        for dev in devs:
            ag_copy(i, h, sent[0], dev).start()
            sent[0] += 1

    def to_sib(i):
        as_copy(i, sent[1]).start()
        sent[1] += 1

    for h in range(2):
        pass_on(b, h, up, down, x2)
    to_sib(b)

    def norm_q(i, _):
        v = q_ref[rows(i), :]
        inv = lax.rsqrt(jnp.sum(v * v, axis=1, keepdims=True) + EPS)
        qh[rows(i), :] = (v * inv).astype(BF16)
        return 0

    q_load.wait()
    lax.fori_loop(0, NQ // NP, norm_q, 0)
    id_load.wait()
    pos_acc[...] = jnp.zeros_like(pos_acc)

    def own(dz, xrel):
        return blk_of(wrap(dz), xh if xrel == 0 else 1 - xh, c)

    sign = 2 * xh - 1

    def got(dz, xrel):
        sides = (dz,) if dz in (0, 4) else (-dz, dz)
        for h in range(2):
            for d in sides:
                i = own(d, xrel)
                ag_copy(i, h, 0, sib).wait_recv()
                if xrel == 0 and dz in CROSS and dz > 0:
                    pass_on(i, h, x2)
                if dz < 3 and (xrel == 0 or dz + 1 not in CROSS):
                    if d <= 0:
                        pass_on(i, h, up)
                    if d >= 0:
                        pass_on(i, h, down)
            if dz == 3 and (xrel == 0 or 4 not in CROSS):
                s = sign if xrel == 0 else -sign
                pass_on(
                    blk_of(wrap(3 * s), xh if xrel == 0 else 1 - xh, c), h, at(wrap(-s), xh, c)
                )
        for d in sides:
            to_sib(own(d, xrel))

    def from_sib(dz):
        for xx in range(2):
            as_copy(blk_of(wrap(dz), xx, 1 - c), 0).wait_recv()

    def gather_turn(t):
        if t == 0:
            got(0, 1)
            got(1, 0)
            from_sib(0)
        if t == 1:
            got(1, 1)
            got(2, 0)
            from_sib(-1)
        if t == 2:
            got(2, 1)
            from_sib(1)
        if t == 3:
            got(3, 0)
            from_sib(-2)
        if t == 4:
            got(3, 1)
            from_sib(2)
        if t == 5:
            from_sib(-3)
        if t == 6:
            got(4, 0)
            got(4, 1)
            from_sib(3)
        if t == 7:
            from_sib(4)

    base = o * (NB * NP)

    def mask_of(zz):
        cols = base + zz * GROUP + lax.broadcasted_iota(jnp.int32, (GROUP, NQ), 0)
        return cols == id_ref[...]

    def first(t, _):
        for k in range(8):
            pl.when(t == k)(lambda k=k: gather_turn(k))
        far_by = lax.div(t + 1, 2)
        zz = wrap(jnp.where(lax.rem(t, 2) == 1, -far_by, far_by))
        pg = pall[rows(zz, GROUP), :]
        s = SHARP2 * dot(pg, qh[...], NT)
        scores[rows(zz, GROUP), :] = s
        row_part[pl.ds(t, 1), :] = lse_of(s, 0)
        pos_acc[...] += jnp.sum(jnp.where(mask_of(zz), s, 0.0), axis=0, keepdims=True)
        st = SHARP2 * dot(qh[...], pg, NT)
        col_part[pl.ds(zz, 1), :] = lse_of(st, 0)
        return 0

    lax.fori_loop(0, 8, first, 0)

    sib_col = copy(col_part, col_sib, cs_ss.at[0], cs_rs.at[0], sib)
    sib_col.start()
    row_lse_part = lse_of(row_part[...], 0)
    pos_part = pos_acc[...]
    for k in range(4):
        row_all[o, k : k + 1, :] = row_lse_part[:, 128 * k : 128 * k + 128]
        row_all[o, 4 + k : 5 + k, :] = pos_part[:, 128 * k : 128 * k + 128]

    def row_copy(k):
        other, dev = outer_peer(k)
        send = copy(row_all.at[o], row_all.at[o], row_ss.at[k], row_rs.at[o], dev)
        recv = copy(row_all.at[o], row_all.at[other], row_ss.at[k], row_rs.at[other], dev)
        return send, recv

    def row_start(k, _):
        row_copy(k)[0].start()
        return 0

    lax.fori_loop(1, NO, row_start, 0)
    sib_col.wait_recv()
    a0, a1 = col_part[...], col_sib[...]
    top = jnp.maximum(a0, a1)
    col_all[chip] = top + jnp.log(jnp.exp2(a0 - top) + jnp.exp2(a1 - top)) * (1.0 / LN2)

    def col_copy(k):
        other, dev = chip_peer(k)
        send = copy(col_all.at[chip], col_all.at[chip], col_ss.at[k], col_rs.at[chip], dev)
        recv = copy(col_all.at[chip], col_all.at[other], col_ss.at[k], col_rs.at[other], dev)
        return send, recv

    def col_start(k, _):
        col_copy(k)[0].start()
        return 0

    lax.fori_loop(1, 16, col_start, 0)

    def row_wait(k, _):
        row_copy(k)[1].wait_recv()
        return 0

    lax.fori_loop(1, NO, row_wait, 0)
    rall = row_all[...]
    row_lse4 = lse_of(rall[:, 0:4, :], 0)[0]
    pos4 = jnp.sum(rall[:, 4:8, :], axis=0)
    row_wide[...] = row_lse4 + 1.0
    sum_r[...] = jnp.broadcast_to(jnp.sum(row_lse4 - 2.0 * pos4, keepdims=True), (8, 128))
    sib_r = copy(sum_r, sum_r_sib, r1_ss.at[0], r1_rs.at[0], sib)
    sib_r.start()

    def col_wait(k, _):
        col_copy(k)[1].wait_recv()
        return 0

    lax.fori_loop(1, 16, col_wait, 0)
    col_lse = lse_of(col_all[...], 0)[0]
    for k in range(NZ):
        col_wide[k * GROUP : (k + 1) * GROUP, :] = jnp.broadcast_to(
            col_lse[k : k + 1, :] + 1.0, (128, GROUP)
        ).T
    sum_c_all[o] = jnp.broadcast_to(jnp.sum(col_lse, keepdims=True), (8, 128))

    def c_copy(k):
        other, dev = outer_peer(k)
        send = copy(sum_c_all.at[o], sum_c_all.at[o], ca_ss.at[k], ca_rs.at[o], dev)
        recv = copy(sum_c_all.at[o], sum_c_all.at[other], ca_ss.at[k], ca_rs.at[other], dev)
        return send, recv

    def q_copy(other):
        dev = (b, other)
        send = copy(q_out.at[other], q_in.at[o], q_ss.at[other], q_rs.at[o], dev)
        recv = copy(q_out.at[other], q_in.at[other], q_ss.at[other], q_rs.at[other], dev)
        return send, recv

    def q_chunk(k, _):
        k = lax.rem(k + lax.div(o, 2), 4)
        lanes = pl.ds(pl.multiple_of(k * 128, 128), 128)
        rl = row_wide[pl.ds(k, 1), :]
        ids = id_ref[:, lanes] - base

        def tile(g, _):
            s = scores[rows(g, GROUP), lanes]
            cols = g * GROUP + lax.broadcasted_iota(jnp.int32, (GROUP, 128), 0)
            w = jnp.exp2(s - rl) + jnp.exp2(s - col_wide[rows(g, GROUP), :])
            weights[rows(g, GROUP), lanes] = (w - jnp.where(cols == ids, 1.0, 0.0)).astype(BF16)
            return 0

        lax.fori_loop(0, NZ, tile, 0)
        g = dot(weights[:, lanes], pall[...], TN)
        for h in range(2):
            other = 2 * k + h
            part = g[h * NP : (h + 1) * NP, :]

            @pl.when(other == o)
            def _():
                q_own[...] = part

            @pl.when(other != o)
            def _():
                q_out[other] = part.astype(BF16)
                q_copy(other)[0].start()

        return 0

    lax.fori_loop(0, 4, q_chunk, 0)

    def sib_copy(i):
        return copy(sib_out.at[i], sib_in.at[i], sib_ss.at[i], sib_rs.at[i], sib)

    def slot(way, d, xx):
        return way * 8 + (d - 1) * 2 + xx

    def ring_copy(way, d, xx, h):
        i = slot(way, d, xx)
        part = pl.ds(h * HALF, HALF)
        return copy(
            ring_out.at[i, part], ring_in.at[i, part],
            ring_ss.at[i * 2 + h], ring_rs.at[i * 2 + h], up if way == 0 else down,
        )

    def arrived(way, d, xx, h):
        ring_copy(way, d, xx, h).wait_recv()
        return ring_in[slot(way, d, xx), h * HALF : (h + 1) * HALF, :].astype(F32)

    def joined(dz, xx, h):
        i = wrap(dz) * 2 + xx
        if h == 0:
            sib_copy(i).wait_recv()
        part = slice(h * HALF, (h + 1) * HALF)
        return mine[i, part, :] + sib_in[i, part, :].astype(F32)

    def ring_send(d, xx_up, carry):
        for h in range(2):
            for way, xx in ((0, xx_up), (1, 1 - xx_up)):
                value = joined(d if way == 0 else -d, xx, h)
                if carry:
                    value = value + arrived(way, d + 1, xx, h)
                ring_out[slot(way, d, xx), h * HALF : (h + 1) * HALF, :] = value.astype(BF16)
                ring_copy(way, d, xx, h).start()

    def second(t, _):
        far_by = 4 - lax.div(t + 1, 2)
        zz = wrap(jnp.where(lax.rem(t, 2) == 1, far_by, -far_by))
        pres[...] = SHARP * dot(weights[rows(zz, GROUP), :], qh[...], NN)
        for xx in range(2):
            i = zz * 2 + xx
            sib_out[i] = pres[rows(xx * 2 + 1 - c), :].astype(BF16)
            sib_copy(i).start()
            mine[i] = pres[rows(xx * 2 + c), :]
        pl.when(t == 1)(lambda: ring_send(4, 0, False))
        pl.when(t == 3)(lambda: ring_send(3, 1, False))
        return 0

    lax.fori_loop(0, 8, second, 0)

    def c_start(k, _):
        c_copy(k)[0].start()
        return 0

    lax.fori_loop(1, NO, c_start, 0)
    ring_send(3, 0, True)
    sib_r.wait_recv()
    sum_r_all[chip] = sum_r[...] + sum_r_sib[...]

    def r_copy(k):
        other, dev = chip_peer(k)
        send = copy(sum_r_all.at[chip], sum_r_all.at[chip], ra_ss.at[k], ra_rs.at[chip], dev)
        recv = copy(sum_r_all.at[chip], sum_r_all.at[other], ra_ss.at[k], ra_rs.at[other], dev)
        return send, recv

    def r_start(k, _):
        r_copy(k)[0].start()
        return 0

    lax.fori_loop(1, 16, r_start, 0)

    def q_add(k, _):
        other, _dev = outer_peer(k)
        q_copy(other)[1].wait_recv()
        q_own[...] += q_in[other].astype(F32)
        return 0

    lax.fori_loop(1, NO, q_add, 0)
    qv = q_ref[rows(o), :]
    q_inv = lax.rsqrt(jnp.sum(qv * qv, axis=1, keepdims=True) + EPS)
    qu = qv * q_inv
    qg = SHARP * q_own[...]
    q_fin[rows(o), :] = (q_inv * (qg - qu * jnp.sum(qu * qg, axis=1, keepdims=True))).astype(BF16)

    def f_copy(k):
        other, dev = outer_peer(k)
        send = copy(q_fin.at[rows(o)], q_fin.at[rows(o)], f_ss.at[k], f_rs.at[o], dev)
        recv = copy(q_fin.at[rows(o)], q_fin.at[rows(other)], f_ss.at[k], f_rs.at[other], dev)
        return send, recv

    def f_start(k, _):
        f_copy(k)[0].start()
        return 0

    lax.fori_loop(1, NO, f_start, 0)

    ring_send(2, 1, True)
    ring_send(2, 0, True)
    ring_send(1, 1, True)
    ring_send(1, 0, True)

    other_i, own_i = z * 2 + 1 - xh, z * 2 + xh

    def total(xx, i, h):
        value = mine[i, h * HALF : (h + 1) * HALF, :] + sib_in[
            i, h * HALF : (h + 1) * HALF, :
        ].astype(F32)
        return value + arrived(0, 1, xx, h) + arrived(1, 1, xx, h)

    def x_copy(h):
        part = pl.ds(h * HALF, HALF)
        return copy(x_out.at[part], x_in.at[part], x_ss.at[h], x_rs.at[h], x2)

    sib_copy(other_i).wait_recv()
    sib_copy(own_i).wait_recv()
    for h in range(2):
        x_out[h * HALF : (h + 1) * HALF, :] = total(1 - xh, other_i, h).astype(BF16)
        x_copy(h).start()
    pg_own = [total(xh, own_i, h) for h in range(2)]

    def c_wait(k, _):
        c_copy(k)[1].wait_recv()
        return 0

    def r_wait(k, _):
        r_copy(k)[1].wait_recv()
        return 0

    lax.fori_loop(1, NO, c_wait, 0)
    lax.fori_loop(1, 16, r_wait, 0)
    loss_ref[...] = (jnp.sum(sum_r_all[...], axis=0) + jnp.sum(sum_c_all[...], axis=0)) * (
        LN2 / (2.0 * NB * NP * NO)
    )

    pu = p_ref[...]
    p_inv2 = lax.rsqrt(jnp.sum(pu * pu, axis=1, keepdims=True) + EPS)
    pu = pu * p_inv2

    for h in range(2):
        part = slice(h * HALF, (h + 1) * HALF)
        x_copy(h).wait_recv()
        g = pg_own[h] + x_in[part, :].astype(F32)
        u = pu[part, :]
        po_ref[part, :] = p_inv2[part, :] * (g - u * jnp.sum(u * g, axis=1, keepdims=True))

    def f_wait(k, _):
        f_copy(k)[1].wait_recv()
        return 0

    lax.fori_loop(1, NO, f_wait, 0)

    def ag_done(k, _):
        ag_copy(b, 0, k, sib).wait_send()
        return 0

    def as_done(k, _):
        as_copy(b, k).wait_send()
        return 0

    lax.fori_loop(0, sent[0], ag_done, 0)
    lax.fori_loop(0, sent[1], as_done, 0)
    sib_col.wait_send()
    sib_r.wait_send()
    for h in range(2):
        x_copy(h).wait_send()

    def outer_done(k, _):
        row_copy(k)[0].wait_send()
        c_copy(k)[0].wait_send()
        f_copy(k)[0].wait_send()
        q_copy(outer_peer(k)[0])[0].wait_send()
        return 0

    lax.fori_loop(1, NO, outer_done, 0)

    def chip_done(k, _):
        col_copy(k)[0].wait_send()
        r_copy(k)[0].wait_send()
        return 0

    lax.fori_loop(1, 16, chip_done, 0)

    def sib_done(k, _):
        sib_copy(k).wait_send()
        return 0

    lax.fori_loop(0, 16, sib_done, 0)
    for way in range(2):
        for d in (1, 2, 3, 4):
            for xx in range(2):
                if d < 4 or xx == way:
                    for h in range(2):
                        ring_copy(way, d, xx, h).wait_send()


def widen(q_ref, p_ref, loss_ref, qo_ref, po_ref, lo_ref):
    qo_ref[...] = q_ref[...].astype(F32)
    po_ref[...] = p_ref[...]
    lo_ref[...] = loss_ref[0:1, 0:1]


def per_device(queries, passages, positive_id):
    vmem = pl.BlockSpec(memory_space=pltpu.VMEM)
    hbm = pl.BlockSpec(memory_space=pl.ANY)
    dma = pltpu.SemaphoreType.DMA
    scratch = [
        pltpu.VMEM((NQ, D), F32),
        pltpu.VMEM((NP, D), F32),
        pltpu.VMEM((1, NQ), jnp.int32),
        dma((3,)),
        pltpu.VMEM((NB * NP, D), BF16),
        pltpu.VMEM((NQ, D), BF16),
        pltpu.VMEM((NB * NP, NQ), F32),
        pltpu.VMEM((NB * NP, NQ), BF16),
        pltpu.VMEM((16, NP, D), F32),
        pltpu.VMEM((GROUP, D), F32),
        pltpu.VMEM((16, NP, D), BF16),
        pltpu.VMEM((16, NP, D), BF16),
        pltpu.VMEM((16, NP, D), BF16),
        pltpu.VMEM((16, NP, D), BF16),
        pltpu.VMEM((NP, D), BF16),
        pltpu.VMEM((NP, D), BF16),
        pltpu.VMEM((NO, NP, D), BF16),
        pltpu.VMEM((NO, NP, D), BF16),
        pltpu.VMEM((NP, D), F32),
        pltpu.VMEM((8, NQ), F32),
        pltpu.VMEM((4, 128), F32),
        pltpu.VMEM((1, NQ), F32),
        pltpu.VMEM((NZ, GROUP), F32),
        pltpu.VMEM((NZ, GROUP), F32),
        pltpu.VMEM((NB * NP, 128), F32),
        pltpu.VMEM((16, NZ, GROUP), F32),
        pltpu.VMEM((NO, 8, 128), F32),
        pltpu.VMEM((8, 128), F32),
        pltpu.VMEM((8, 128), F32),
        pltpu.VMEM((16, 8, 128), F32),
        pltpu.VMEM((NO, 8, 128), F32),
        dma((64,)), dma((2 * NB,)), dma((16,)),
        dma((1,)), dma((1,)),
        dma((16,)), dma((16,)),
        dma((NO,)), dma((NO,)),
        dma((16,)), dma((16,)),
        dma((32,)), dma((32,)),
        dma((2,)), dma((2,)),
        dma((NO,)), dma((NO,)),
        dma((NO,)), dma((NO,)),
        dma((1,)), dma((1,)),
        dma((16,)), dma((16,)),
        dma((NO,)), dma((NO,)),
    ]
    qd, pd, loss = pl.pallas_call(
        kernel,
        out_shape=(
            jax.ShapeDtypeStruct((NQ, D), BF16),
            jax.ShapeDtypeStruct((NP, D), F32),
            jax.ShapeDtypeStruct((8, 128), F32),
        ),
        in_specs=[hbm, hbm, hbm],
        out_specs=(vmem, vmem, vmem),
        scratch_shapes=scratch,
        compiler_params=pltpu.CompilerParams(
            collective_id=0, has_side_effects=True, vmem_limit_bytes=56 * 2**20
        ),
    )(queries, passages, positive_id.reshape(1, NQ))
    parts = 2
    return pl.pallas_call(
        widen,
        grid=(parts,),
        out_shape=(
            jax.ShapeDtypeStruct((NQ, D), F32),
            jax.ShapeDtypeStruct((NP, D), F32),
            jax.ShapeDtypeStruct((1, 1), F32),
        ),
        in_specs=[
            pl.BlockSpec((NQ // parts, D), lambda i: (i, 0)),
            pl.BlockSpec((NP // parts, D), lambda i: (i, 0)),
            pl.BlockSpec((8, 128), lambda i: (0, 0)),
        ],
        out_specs=(
            pl.BlockSpec((NQ // parts, D), lambda i: (i, 0)),
            pl.BlockSpec((NP // parts, D), lambda i: (i, 0)),
            pl.BlockSpec((1, 1), lambda i: (0, 0)),
        ),
    )(qd, pd, loss)


def solution(mesh):
    def step(queries, passages, positive_id):
        qd, pd, loss = per_device(queries, passages, positive_id)
        return qd, pd, loss.reshape(())

    placed = (P("blk", None), P(("outer", "blk"), None), P("blk"))
    return jax.shard_map(
        step,
        mesh=mesh,
        in_specs=placed,
        out_specs=(P("blk", None), P(("outer", "blk"), None), P()),
        check_vma=False,
    )
```

```python
import jax
import jax.numpy as jnp
from jax import lax
from jax.experimental import pallas as pl
from jax.experimental.pallas import tpu as pltpu
from jax.sharding import PartitionSpec as P

MESH = pl.DeviceIdType.MESH
SHARP = 125.0
EPS = 1e-06
LN2 = 0.6931471805599453
SHARP2 = SHARP / LN2
HALF = 32
CROSS = (0, 1)
ORDER = (
    ((0, 1), (1, 0)), ((1, 1), (2, 0)), ((2, 1),), ((3, 0),), ((3, 1),), (), ((4, 0), (4, 1)), (),
)
D = 1024
NQ = 512
NP = 64
NB = 32
NO = 8
NZ = 8
GROUP = 4 * NP
F32 = jnp.float32
BF16 = jnp.bfloat16
NT = (((1,), (1,)), ((), ()))
NN = (((1,), (0,)), ((), ()))
TN = (((0,), (0,)), ((), ()))


def dot(a, b, dims):
    return lax.dot_general(a, b, dims, preferred_element_type=F32)


def lse_of(parts, axis):
    top = jnp.max(parts, axis=axis, keepdims=True)
    return top + jnp.log(jnp.sum(jnp.exp2(parts - top), axis=axis, keepdims=True)) * (1.0 / LN2)


def kernel(
    q_any, p_any, id_any,
    q_fin, po_ref, loss_ref,
    q_ref, p_ref, id_ref, in_sem,
    pall, qh, scores, weights, mine, pres, sib_out, sib_in, ring_out, ring_in,
    x_out, x_in, q_out, q_in, q_own, q_done_rows, own_sem,
    row_part, row_wide, pos_acc, col_part, col_sib, col_wide, col_all, row_all,
    sum_r, sum_r_sib, sum_r_all, sum_c_all,
    ag_ss, ag_rs, as_ss, cs_ss, cs_rs, col_ss, col_rs, row_ss, row_rs,
    sib_ss, sib_rs, ring_ss, ring_rs, x_ss, x_rs, q_ss, q_rs, f_ss, f_rs,
    r1_ss, r1_rs, ra_ss, ra_rs, ca_ss, ca_rs,
):
    b = lax.axis_index("blk")
    o = lax.axis_index("outer")
    c = lax.rem(b, 2)
    xh = lax.rem(lax.div(b, 2), 2)
    z = lax.div(b, 4)
    chip = z * 2 + xh

    def blk_of(zz, xx, cc):
        return (zz * 2 + xx) * 2 + cc

    def wrap(dz):
        return lax.rem(z + dz + 16, NZ)

    y = lax.rem(o, 4)
    xl = lax.div(o, 4)

    def outer_of(xx):
        return lax.rem(xl + xx + xh, 2) * 4 + y

    def at(zz, xx, cc):
        return (blk_of(zz, xx, cc), outer_of(xx))

    sib = at(z, xh, 1 - c)
    x2 = at(z, 1 - xh, c)
    up = at(wrap(1), xh, c)
    down = at(wrap(-1), xh, c)

    def chip_peer(k):
        other = lax.rem(chip + k, 16)
        return other, (other * 2 + c, outer_of(lax.rem(other, 2)))

    def outer_peer(k):
        other = lax.rem(o + k, NO)
        return other, (b, other)

    def copy(src, dst, ss, rs, dev):
        return pltpu.make_async_remote_copy(
            src_ref=src, dst_ref=dst, send_sem=ss, recv_sem=rs, device_id=dev, device_id_type=MESH
        )

    p_load = pltpu.make_async_copy(p_any, p_ref, in_sem.at[0])
    q_load = pltpu.make_async_copy(q_any, q_ref, in_sem.at[1])
    id_load = pltpu.make_async_copy(id_any, id_ref, in_sem.at[2])
    p_load.start()
    barrier = pltpu.get_barrier_semaphore()
    for dev in (x2, up, down, sib):
        pl.semaphore_signal(barrier, inc=1, device_id=dev, device_id_type=MESH)

    def greet_outer(k, _):
        pl.semaphore_signal(barrier, inc=1, device_id=outer_peer(k)[1], device_id_type=MESH)
        return 0

    lax.fori_loop(1, NO, greet_outer, 0)
    q_load.start()
    id_load.start()

    def rows(i, n=NP):
        return pl.ds(pl.multiple_of(i * n, n), n)

    def shard(i):
        return pall.at[rows(i)]

    p_load.wait()
    pv = p_ref[...]
    p_inv = lax.rsqrt(jnp.sum(pv * pv, axis=1, keepdims=True) + EPS)
    pall[rows(b), :] = (pv * p_inv).astype(BF16)
    pl.semaphore_wait(barrier, 4 + NO - 1)

    def piece(i, h):
        return pall.at[pl.ds(pl.multiple_of(i * NP + h * HALF, HALF), HALF)]

    def ag_copy(i, h, k, dev):
        return copy(piece(i, h), piece(i, h), ag_ss.at[k], ag_rs.at[i * 2 + h], dev)

    def as_copy(i, k):
        return copy(shard(i), shard(i), as_ss.at[k], ag_rs.at[i * 2], sib)

    sent = [0, 0]

    def pass_on(i, h, *devs):
        for dev in devs:
            ag_copy(i, h, sent[0], dev).start()
            sent[0] += 1

    def to_sib(i):
        as_copy(i, sent[1]).start()
        sent[1] += 1

    for h in range(2):
        pass_on(b, h, up, down, x2)
    to_sib(b)

    def norm_q(i, _):
        v = q_ref[rows(i), :]
        inv = lax.rsqrt(jnp.sum(v * v, axis=1, keepdims=True) + EPS)
        qh[rows(i), :] = (v * inv).astype(BF16)
        return 0

    q_load.wait()
    lax.fori_loop(0, NQ // NP, norm_q, 0)
    id_load.wait()
    pos_acc[...] = jnp.zeros_like(pos_acc)

    def own(dz, xrel):
        return blk_of(wrap(dz), xh if xrel == 0 else 1 - xh, c)

    sign = 2 * xh - 1

    def got(dz, xrel):
        sides = (dz,) if dz in (0, 4) else (-dz, dz)
        for h in range(2):
            for d in sides:
                i = own(d, xrel)
                ag_copy(i, h, 0, sib).wait_recv()
                if xrel == 0 and dz in CROSS and dz > 0:
                    pass_on(i, h, x2)
                if dz < 3 and (xrel == 0 or dz + 1 not in CROSS):
                    if d <= 0:
                        pass_on(i, h, up)
                    if d >= 0:
                        pass_on(i, h, down)
            if dz == 3 and (xrel == 0 or 4 not in CROSS):
                s = sign if xrel == 0 else -sign
                pass_on(
                    blk_of(wrap(3 * s), xh if xrel == 0 else 1 - xh, c), h, at(wrap(-s), xh, c)
                )
        for d in sides:
            to_sib(own(d, xrel))

    def from_sib(dz):
        for xx in range(2):
            as_copy(blk_of(wrap(dz), xx, 1 - c), 0).wait_recv()

    def gather_turn(t):
        for k, step in enumerate(ORDER):
            if t == k:
                for dz, xrel in step:
                    got(dz, xrel)
        from_sib((0, -1, 1, -2, 2, -3, 3, 4)[t])

    base = [outer_of(xx) * (NB * NP) for xx in range(2)]

    def mask_of(zz):
        row = lax.broadcasted_iota(jnp.int32, (GROUP, NQ), 0)
        return row + zz * GROUP + jnp.where(row < GROUP // 2, base[0], base[1]) == id_ref[...]

    def first(t, _):
        for k in range(8):
            pl.when(t == k)(lambda k=k: gather_turn(k))
        far_by = lax.div(t + 1, 2)
        zz = wrap(jnp.where(lax.rem(t, 2) == 1, -far_by, far_by))
        pg = pall[rows(zz, GROUP), :]
        s = SHARP2 * dot(pg, qh[...], NT)
        scores[rows(zz, GROUP), :] = s
        row_part[pl.ds(t, 1), :] = lse_of(s, 0)
        pos_acc[...] += jnp.sum(jnp.where(mask_of(zz), s, 0.0), axis=0, keepdims=True)
        st = SHARP2 * dot(qh[...], pg, NT)
        col_part[pl.ds(zz, 1), :] = lse_of(st, 0)
        return 0

    lax.fori_loop(0, 8, first, 0)

    sib_col = copy(col_part, col_sib, cs_ss.at[0], cs_rs.at[0], sib)
    sib_col.start()
    row_lse_part = lse_of(row_part[...], 0)
    pos_part = pos_acc[...]
    for k in range(4):
        row_all[o, k : k + 1, :] = row_lse_part[:, 128 * k : 128 * k + 128]
        row_all[o, 4 + k : 5 + k, :] = pos_part[:, 128 * k : 128 * k + 128]

    def row_copy(k):
        other, dev = outer_peer(k)
        send = copy(row_all.at[o], row_all.at[o], row_ss.at[k], row_rs.at[o], dev)
        recv = copy(row_all.at[o], row_all.at[other], row_ss.at[k], row_rs.at[other], dev)
        return send, recv

    def row_start(k, _):
        row_copy(k)[0].start()
        return 0

    lax.fori_loop(1, NO, row_start, 0)
    sib_col.wait_recv()
    a0, a1 = col_part[...], col_sib[...]
    top = jnp.maximum(a0, a1)
    col_all[chip] = top + jnp.log(jnp.exp2(a0 - top) + jnp.exp2(a1 - top)) * (1.0 / LN2)

    def col_copy(k):
        other, dev = chip_peer(k)
        send = copy(col_all.at[chip], col_all.at[chip], col_ss.at[k], col_rs.at[chip], dev)
        recv = copy(col_all.at[chip], col_all.at[other], col_ss.at[k], col_rs.at[other], dev)
        return send, recv

    def col_start(k, _):
        col_copy(k)[0].start()
        return 0

    lax.fori_loop(1, 16, col_start, 0)

    def row_wait(k, _):
        row_copy(k)[1].wait_recv()
        return 0

    lax.fori_loop(1, NO, row_wait, 0)
    rall = row_all[...]
    row_lse4 = lse_of(rall[:, 0:4, :], 0)[0]
    pos4 = jnp.sum(rall[:, 4:8, :], axis=0)
    for k in range(4):
        row_wide[:, 128 * k : 128 * k + 128] = row_lse4[k : k + 1, :] + 1.0
    sum_r[...] = jnp.broadcast_to(jnp.sum(row_lse4 - 2.0 * pos4, keepdims=True), (8, 128))
    sib_r = copy(sum_r, sum_r_sib, r1_ss.at[0], r1_rs.at[0], sib)
    sib_r.start()

    def col_wait(k, _):
        col_copy(k)[1].wait_recv()
        return 0

    lax.fori_loop(1, 16, col_wait, 0)
    col_lse = lse_of(col_all[...], 0)[0]
    for k in range(NZ):
        col_wide[k * GROUP : (k + 1) * GROUP, :] = jnp.broadcast_to(
            col_lse[k : k + 1, :] + 1.0, (128, GROUP)
        ).T
    def passage_set(oo):
        return lax.rem(lax.div(oo, 4) + xh, 2) * 4 + lax.rem(oo, 4)

    sum_c_all[passage_set(o)] = jnp.broadcast_to(jnp.sum(col_lse, keepdims=True), (8, 128))

    def c_copy(k):
        other, dev = outer_peer(k)
        me, it = passage_set(o), passage_set(other)
        send = copy(sum_c_all.at[me], sum_c_all.at[me], ca_ss.at[k], ca_rs.at[me], dev)
        recv = copy(sum_c_all.at[me], sum_c_all.at[it], ca_ss.at[k], ca_rs.at[it], dev)
        return send, recv

    def tile(g, _):
        s = scores[rows(g, GROUP), :]
        cl = col_wide[rows(g, GROUP), :]
        w = jnp.exp2(s - row_wide[...]) + jnp.exp2(s - jnp.concatenate([cl] * 4, axis=1))
        weights[rows(g, GROUP), :] = (w - jnp.where(mask_of(g), 1.0, 0.0)).astype(BF16)
        return 0

    lax.fori_loop(0, NZ, tile, 0)

    def q_copy(st, other):
        dev = (b, other)
        i, mine_i = st * NO + other, st * NO + o
        send = copy(q_out.at[i], q_in.at[mine_i], q_ss.at[i], q_rs.at[mine_i], dev)
        recv = copy(q_out.at[i], q_in.at[i], q_ss.at[i], q_rs.at[i], dev)
        return send, recv

    def q_stage(st):
        g = dot(weights[:, st * 256 : (st + 1) * 256], pall[...], TN)
        for other in range(NO):
            part = g[other * HALF : (other + 1) * HALF, :]

            @pl.when(other == o)
            def _():
                q_own[st] = part

            @pl.when(other != o)
            def _():
                q_out[st * NO + other] = part.astype(BF16)
                q_copy(st, other)[0].start()

    def sib_copy(i):
        return copy(sib_out.at[i], sib_in.at[i], sib_ss.at[i], sib_rs.at[i], sib)

    def slot(way, d, xx):
        return way * 8 + (d - 1) * 2 + xx

    def ring_copy(way, d, xx, h):
        i = slot(way, d, xx)
        part = pl.ds(h * HALF, HALF)
        return copy(
            ring_out.at[i, part], ring_in.at[i, part],
            ring_ss.at[i * 2 + h], ring_rs.at[i * 2 + h], up if way == 0 else down,
        )

    def arrived(way, d, xx, h):
        ring_copy(way, d, xx, h).wait_recv()
        return ring_in[slot(way, d, xx), h * HALF : (h + 1) * HALF, :].astype(F32)

    def joined(dz, xx, h):
        i = wrap(dz) * 2 + xx
        if h == 0:
            sib_copy(i).wait_recv()
        part = slice(h * HALF, (h + 1) * HALF)
        return mine[i, part, :] + sib_in[i, part, :].astype(F32)

    def ring_send(d, xx_up, carry):
        for h in range(2):
            for way, xx in ((0, xx_up), (1, 1 - xx_up)):
                value = joined(d if way == 0 else -d, xx, h)
                if carry:
                    value = value + arrived(way, d + 1, xx, h)
                ring_out[slot(way, d, xx), h * HALF : (h + 1) * HALF, :] = value.astype(BF16)
                ring_copy(way, d, xx, h).start()

    def second(t, _):
        pl.when(t == 3)(lambda: q_stage(0))
        far_by = 4 - lax.div(t + 1, 2)
        zz = wrap(jnp.where(lax.rem(t, 2) == 1, far_by, -far_by))
        pres[...] = SHARP * dot(weights[rows(zz, GROUP), :], qh[...], NN)
        for xx in range(2):
            i = zz * 2 + xx
            sib_out[i] = pres[rows(xx * 2 + 1 - c), :].astype(BF16)
            sib_copy(i).start()
            mine[i] = pres[rows(xx * 2 + c), :]
        pl.when(t == 1)(lambda: ring_send(4, 0, False))
        pl.when(t == 3)(lambda: ring_send(3, 1, False))
        return 0

    lax.fori_loop(0, 8, second, 0)
    q_stage(1)
    ring_send(3, 0, True)

    def c_start(k, _):
        c_copy(k)[0].start()
        return 0

    lax.fori_loop(1, NO, c_start, 0)
    sib_r.wait_recv()
    sum_r_all[chip] = sum_r[...] + sum_r_sib[...]

    def r_copy(k):
        other, dev = chip_peer(k)
        send = copy(sum_r_all.at[chip], sum_r_all.at[chip], ra_ss.at[k], ra_rs.at[chip], dev)
        recv = copy(sum_r_all.at[chip], sum_r_all.at[other], ra_ss.at[k], ra_rs.at[other], dev)
        return send, recv

    def r_start(k, _):
        r_copy(k)[0].start()
        return 0

    lax.fori_loop(1, 16, r_start, 0)

    def ag_done(k, _):
        ag_copy(b, 0, k, sib).wait_send()
        return 0

    def as_done(k, _):
        as_copy(b, k).wait_send()
        return 0

    def row_done(k, _):
        row_copy(k)[0].wait_send()
        return 0

    def col_done(k, _):
        col_copy(k)[0].wait_send()
        return 0

    lax.fori_loop(0, sent[0], ag_done, 0)
    lax.fori_loop(0, sent[1], as_done, 0)
    lax.fori_loop(1, NO, row_done, 0)
    lax.fori_loop(1, 16, col_done, 0)
    sib_col.wait_send()
    sib_r.wait_send()
    ring_send(2, 1, True)
    ring_send(2, 0, True)

    def sib_done(k, _):
        sib_copy(k).wait_send()
        return 0

    lax.fori_loop(0, 16, sib_done, 0)

    def q_rows(st, other):
        return pl.ds(pl.multiple_of(st * 256 + other * HALF, HALF), HALF)

    def f_copy(st, k):
        other, dev = outer_peer(k)
        here, there = q_fin.at[q_rows(st, o)], q_fin.at[q_rows(st, other)]
        send = copy(q_done_rows.at[st], here, f_ss.at[st * NO + k], f_rs.at[st * NO + o], dev)
        recv = copy(q_done_rows.at[st], there, f_ss.at[st * NO + k], f_rs.at[st * NO + other], dev)
        return send, recv

    def f_own(st):
        return pltpu.make_async_copy(q_done_rows.at[st], q_fin.at[q_rows(st, o)], own_sem.at[st])

    def q_finish(st):
        def q_add(k, _):
            other, _dev = outer_peer(k)
            q_copy(st, other)[1].wait_recv()
            q_own[st] += q_in[st * NO + other].astype(F32)
            return 0

        lax.fori_loop(1, NO, q_add, 0)
        qv = q_ref[q_rows(st, o), :]
        q_inv = lax.rsqrt(jnp.sum(qv * qv, axis=1, keepdims=True) + EPS)
        qu = qv * q_inv
        qg = SHARP * q_own[st]
        q_done_rows[st] = (
            q_inv * (qg - qu * jnp.sum(qu * qg, axis=1, keepdims=True))
        ).astype(BF16)

        def f_start(k, _):
            f_copy(st, k)[0].start()
            return 0

        lax.fori_loop(1, NO, f_start, 0)
        f_own(st).start()

    q_finish(0)
    ring_send(1, 1, True)
    ring_send(1, 0, True)
    for way in range(2):
        for d, xx in ((4, way), (3, 0), (3, 1)):
            for h in range(2):
                ring_copy(way, d, xx, h).wait_send()
    q_finish(1)

    def q_done(k, _):
        for st in range(2):
            q_copy(st, outer_peer(k)[0])[0].wait_send()
        return 0

    lax.fori_loop(1, NO, q_done, 0)

    other_i, own_i = z * 2 + 1 - xh, z * 2 + xh

    def total(xx, i, h):
        value = mine[i, h * HALF : (h + 1) * HALF, :] + sib_in[
            i, h * HALF : (h + 1) * HALF, :
        ].astype(F32)
        return value + arrived(0, 1, xx, h) + arrived(1, 1, xx, h)

    def x_copy(h):
        part = pl.ds(h * HALF, HALF)
        return copy(x_out.at[part], x_in.at[part], x_ss.at[h], x_rs.at[h], x2)

    sib_copy(other_i).wait_recv()
    sib_copy(own_i).wait_recv()
    for h in range(2):
        x_out[h * HALF : (h + 1) * HALF, :] = total(1 - xh, other_i, h).astype(BF16)
        x_copy(h).start()
    pg_own = [total(xh, own_i, h) for h in range(2)]

    def c_wait(k, _):
        c_copy(k)[1].wait_recv()
        return 0

    def r_wait(k, _):
        r_copy(k)[1].wait_recv()
        return 0

    lax.fori_loop(1, NO, c_wait, 0)
    lax.fori_loop(1, 16, r_wait, 0)
    loss_ref[...] = (jnp.sum(sum_r_all[...], axis=0) + jnp.sum(sum_c_all[...], axis=0)) * (
        LN2 / (2.0 * NB * NP * NO)
    )

    pu = p_ref[...]
    p_inv2 = lax.rsqrt(jnp.sum(pu * pu, axis=1, keepdims=True) + EPS)
    pu = pu * p_inv2

    for h in range(2):
        part = slice(h * HALF, (h + 1) * HALF)
        x_copy(h).wait_recv()
        g = pg_own[h] + x_in[part, :].astype(F32)
        u = pu[part, :]
        po_ref[part, :] = p_inv2[part, :] * (g - u * jnp.sum(u * g, axis=1, keepdims=True))

    def f_wait(k, _):
        f_copy(0, k)[1].wait_recv()
        f_copy(1, k)[1].wait_recv()
        return 0

    lax.fori_loop(1, NO, f_wait, 0)

    for h in range(2):
        x_copy(h).wait_send()

    def outer_done(k, _):
        c_copy(k)[0].wait_send()
        for st in range(2):
            f_copy(st, k)[0].wait_send()
        return 0

    lax.fori_loop(1, NO, outer_done, 0)

    def chip_done(k, _):
        r_copy(k)[0].wait_send()
        return 0

    lax.fori_loop(1, 16, chip_done, 0)
    for way in range(2):
        for d in (1, 2):
            for xx in range(2):
                for h in range(2):
                    ring_copy(way, d, xx, h).wait_send()
    for st in range(2):
        f_own(st).wait()


def widen(q_ref, p_ref, loss_ref, qo_ref, po_ref, lo_ref):
    qo_ref[...] = q_ref[...].astype(F32)
    po_ref[...] = p_ref[...]
    lo_ref[...] = loss_ref[0:1, 0:1]


def per_device(queries, passages, positive_id):
    vmem = pl.BlockSpec(memory_space=pltpu.VMEM)
    hbm = pl.BlockSpec(memory_space=pl.ANY)
    dma = pltpu.SemaphoreType.DMA
    scratch = [
        pltpu.VMEM((NQ, D), F32),
        pltpu.VMEM((NP, D), F32),
        pltpu.VMEM((1, NQ), jnp.int32),
        dma((3,)),
        pltpu.VMEM((NB * NP, D), BF16),
        pltpu.VMEM((NQ, D), BF16),
        pltpu.VMEM((NB * NP, NQ), F32),
        pltpu.VMEM((NB * NP, NQ), BF16),
        pltpu.VMEM((16, NP, D), F32),
        pltpu.VMEM((GROUP, D), F32),
        pltpu.VMEM((16, NP, D), BF16),
        pltpu.VMEM((16, NP, D), BF16),
        pltpu.VMEM((16, NP, D), BF16),
        pltpu.VMEM((16, NP, D), BF16),
        pltpu.VMEM((NP, D), BF16),
        pltpu.VMEM((NP, D), BF16),
        pltpu.VMEM((2 * NO, HALF, D), BF16),
        pltpu.VMEM((2 * NO, HALF, D), BF16),
        pltpu.VMEM((2, HALF, D), F32),
        pltpu.VMEM((2, HALF, D), BF16),
        dma((2,)),
        pltpu.VMEM((8, NQ), F32),
        pltpu.VMEM((1, NQ), F32),
        pltpu.VMEM((1, NQ), F32),
        pltpu.VMEM((NZ, GROUP), F32),
        pltpu.VMEM((NZ, GROUP), F32),
        pltpu.VMEM((NB * NP, 128), F32),
        pltpu.VMEM((16, NZ, GROUP), F32),
        pltpu.VMEM((NO, 8, 128), F32),
        pltpu.VMEM((8, 128), F32),
        pltpu.VMEM((8, 128), F32),
        pltpu.VMEM((16, 8, 128), F32),
        pltpu.VMEM((NO, 8, 128), F32),
        dma((64,)), dma((2 * NB,)), dma((16,)),
        dma((1,)), dma((1,)),
        dma((16,)), dma((16,)),
        dma((NO,)), dma((NO,)),
        dma((16,)), dma((16,)),
        dma((32,)), dma((32,)),
        dma((2,)), dma((2,)),
        dma((2 * NO,)), dma((2 * NO,)),
        dma((2 * NO,)), dma((2 * NO,)),
        dma((1,)), dma((1,)),
        dma((16,)), dma((16,)),
        dma((NO,)), dma((NO,)),
    ]
    qd, pd, loss = pl.pallas_call(
        kernel,
        out_shape=(
            jax.ShapeDtypeStruct((NQ, D), BF16),
            jax.ShapeDtypeStruct((NP, D), F32),
            jax.ShapeDtypeStruct((8, 128), F32),
        ),
        in_specs=[hbm, hbm, hbm],
        out_specs=(hbm, vmem, vmem),
        scratch_shapes=scratch,
        compiler_params=pltpu.CompilerParams(
            collective_id=0, has_side_effects=True, vmem_limit_bytes=56 * 2**20
        ),
    )(queries, passages, positive_id.reshape(1, NQ))
    parts = 2
    return pl.pallas_call(
        widen,
        grid=(parts,),
        out_shape=(
            jax.ShapeDtypeStruct((NQ, D), F32),
            jax.ShapeDtypeStruct((NP, D), F32),
            jax.ShapeDtypeStruct((1, 1), F32),
        ),
        in_specs=[
            pl.BlockSpec((NQ // parts, D), lambda i: (i, 0)),
            pl.BlockSpec((NP // parts, D), lambda i: (i, 0)),
            pl.BlockSpec((8, 128), lambda i: (0, 0)),
        ],
        out_specs=(
            pl.BlockSpec((NQ // parts, D), lambda i: (i, 0)),
            pl.BlockSpec((NP // parts, D), lambda i: (i, 0)),
            pl.BlockSpec((1, 1), lambda i: (0, 0)),
        ),
    )(qd, pd, loss)


def solution(mesh):
    def step(queries, passages, positive_id):
        qd, pd, loss = per_device(queries, passages, positive_id)
        return qd, pd, loss.reshape(())

    placed = (P("blk", None), P(("outer", "blk"), None), P("blk"))
    return jax.shard_map(
        step,
        mesh=mesh,
        in_specs=placed,
        out_specs=(P("blk", None), P(("outer", "blk"), None), P()),
        check_vma=False,
    )
```

```python
import jax
import jax.numpy as jnp
from jax import lax
from jax.experimental import pallas as pl
from jax.experimental.pallas import tpu as pltpu
from jax.sharding import PartitionSpec as P

MESH = pl.DeviceIdType.MESH
SHARP = 125.0
EPS = 1e-06
LN2 = 0.6931471805599453
SHARP2 = SHARP / LN2
HALF = 32
CROSS = (0, 1)
ORDER = (
    ((0, 1), (1, 0)), ((1, 1), (2, 0)), ((2, 1),), ((3, 0),), ((3, 1),), (), ((4, 0), (4, 1)), (),
)
D = 1024
NQ = 512
NP = 64
NB = 32
NO = 8
NZ = 8
GROUP = 4 * NP
F32 = jnp.float32
BF16 = jnp.bfloat16
NT = (((1,), (1,)), ((), ()))
NN = (((1,), (0,)), ((), ()))
TN = (((0,), (0,)), ((), ()))


def dot(a, b, dims):
    return lax.dot_general(a, b, dims, preferred_element_type=F32)


def lse_of(parts, axis):
    top = jnp.max(parts, axis=axis, keepdims=True)
    return top + jnp.log(jnp.sum(jnp.exp2(parts - top), axis=axis, keepdims=True)) * (1.0 / LN2)


def kernel(
    q_any, p_any, id_any,
    q_fin, po_ref, loss_ref,
    q_ref, p_ref, id_ref, in_sem,
    pall, qh, scores, weights, mine, pres, sib_out, sib_in, ring_out, ring_in,
    x_out, x_in, q_out, q_in, q_own, q_done_rows, own_sem,
    row_part, row_wide, pos_acc, col_part, col_sib, col_wide, col_all, row_all,
    sum_r, sum_r_sib, sum_r_all, sum_c_all,
    ag_ss, ag_rs, as_ss, cs_ss, cs_rs, col_ss, col_rs, row_ss, row_rs,
    sib_ss, sib_rs, ring_ss, ring_rs, x_ss, x_rs, q_ss, q_rs, f_ss, f_rs,
    r1_ss, r1_rs, ra_ss, ra_rs, ca_ss, ca_rs,
):
    b = lax.axis_index("blk")
    o = lax.axis_index("outer")
    c = lax.rem(b, 2)
    xh = lax.rem(lax.div(b, 2), 2)
    z = lax.div(b, 4)
    chip = z * 2 + xh

    def blk_of(zz, xx, cc):
        return (zz * 2 + xx) * 2 + cc

    def wrap(dz):
        return lax.rem(z + dz + 16, NZ)

    y = lax.rem(o, 4)
    xl = lax.div(o, 4)

    def outer_of(xx):
        return lax.rem(xl + xx + xh, 2) * 4 + y

    def at(zz, xx, cc):
        return (blk_of(zz, xx, cc), outer_of(xx))

    sib = at(z, xh, 1 - c)
    x2 = at(z, 1 - xh, c)
    up = at(wrap(1), xh, c)
    down = at(wrap(-1), xh, c)

    def chip_peer(k):
        other = lax.rem(chip + k, 16)
        return other, (other * 2 + c, outer_of(lax.rem(other, 2)))

    def outer_peer(k):
        other = lax.rem(o + k, NO)
        return other, (b, other)

    def copy(src, dst, ss, rs, dev):
        return pltpu.make_async_remote_copy(
            src_ref=src, dst_ref=dst, send_sem=ss, recv_sem=rs, device_id=dev, device_id_type=MESH
        )

    p_load = pltpu.make_async_copy(p_any, p_ref, in_sem.at[0])
    q_load = pltpu.make_async_copy(q_any, q_ref, in_sem.at[1])
    id_load = pltpu.make_async_copy(id_any, id_ref, in_sem.at[2])
    p_load.start()
    barrier = pltpu.get_barrier_semaphore()
    for dev in (x2, up, down, sib):
        pl.semaphore_signal(barrier, inc=1, device_id=dev, device_id_type=MESH)

    def greet_outer(k, _):
        pl.semaphore_signal(barrier, inc=1, device_id=outer_peer(k)[1], device_id_type=MESH)
        return 0

    lax.fori_loop(1, NO, greet_outer, 0)
    q_load.start()
    id_load.start()

    def rows(i, n=NP):
        return pl.ds(pl.multiple_of(i * n, n), n)

    def shard(i):
        return pall.at[rows(i)]

    p_load.wait()
    pv = p_ref[...]
    p_inv = lax.rsqrt(jnp.sum(pv * pv, axis=1, keepdims=True) + EPS)
    pall[rows(b), :] = (pv * p_inv).astype(BF16)
    pl.semaphore_wait(barrier, 4 + NO - 1)

    def piece(i, h):
        return pall.at[pl.ds(pl.multiple_of(i * NP + h * HALF, HALF), HALF)]

    def ag_copy(i, h, k, dev):
        return copy(piece(i, h), piece(i, h), ag_ss.at[k], ag_rs.at[i * 2 + h], dev)

    def as_copy(i, k):
        return copy(shard(i), shard(i), as_ss.at[k], ag_rs.at[i * 2], sib)

    sent = [0, 0]

    def pass_on(i, h, *devs):
        for dev in devs:
            ag_copy(i, h, sent[0], dev).start()
            sent[0] += 1

    def to_sib(i):
        as_copy(i, sent[1]).start()
        sent[1] += 1

    for h in range(2):
        pass_on(b, h, up, down, x2)
    to_sib(b)

    def norm_q(i, _):
        v = q_ref[rows(i), :]
        inv = lax.rsqrt(jnp.sum(v * v, axis=1, keepdims=True) + EPS)
        qh[rows(i), :] = (v * inv).astype(BF16)
        return 0

    q_load.wait()
    lax.fori_loop(0, NQ // NP, norm_q, 0)
    id_load.wait()
    pos_acc[...] = jnp.zeros_like(pos_acc)

    def own(dz, xrel):
        return blk_of(wrap(dz), xh if xrel == 0 else 1 - xh, c)

    sign = 2 * xh - 1

    def got(dz, xrel):
        sides = (dz,) if dz in (0, 4) else (-dz, dz)
        for h in range(2):
            for d in sides:
                i = own(d, xrel)
                ag_copy(i, h, 0, sib).wait_recv()
                if xrel == 0 and dz in CROSS and dz > 0:
                    pass_on(i, h, x2)
                if dz < 3 and (xrel == 0 or dz + 1 not in CROSS):
                    if d <= 0:
                        pass_on(i, h, up)
                    if d >= 0:
                        pass_on(i, h, down)
            if dz == 3 and (xrel == 0 or 4 not in CROSS):
                s = sign if xrel == 0 else -sign
                pass_on(
                    blk_of(wrap(3 * s), xh if xrel == 0 else 1 - xh, c), h, at(wrap(-s), xh, c)
                )
        for d in sides:
            to_sib(own(d, xrel))

    def from_sib(dz):
        for xx in range(2):
            as_copy(blk_of(wrap(dz), xx, 1 - c), 0).wait_recv()

    def gather_turn(t):
        for k, step in enumerate(ORDER):
            if t == k:
                for dz, xrel in step:
                    got(dz, xrel)
        from_sib((0, -1, 1, -2, 2, -3, 3, 4)[t])

    base = [outer_of(xx) * (NB * NP) for xx in range(2)]

    def mask_of(zz):
        row = lax.broadcasted_iota(jnp.int32, (GROUP, NQ), 0)
        return row + zz * GROUP + jnp.where(row < GROUP // 2, base[0], base[1]) == id_ref[...]

    def first(t, _):
        for k in range(8):
            pl.when(t == k)(lambda k=k: gather_turn(k))
        far_by = lax.div(t + 1, 2)
        zz = wrap(jnp.where(lax.rem(t, 2) == 1, -far_by, far_by))
        pg = pall[rows(zz, GROUP), :]
        s = SHARP2 * dot(pg, qh[...], NT)
        scores[rows(zz, GROUP), :] = s
        row_part[pl.ds(t, 1), :] = lse_of(s, 0)
        pos_acc[...] += jnp.sum(jnp.where(mask_of(zz), s, 0.0), axis=0, keepdims=True)
        st = SHARP2 * dot(qh[...], pg, NT)
        col_part[pl.ds(zz, 1), :] = lse_of(st, 0)
        return 0

    lax.fori_loop(0, 8, first, 0)

    sib_col = copy(col_part, col_sib, cs_ss.at[0], cs_rs.at[0], sib)
    sib_col.start()
    row_lse_part = lse_of(row_part[...], 0)
    pos_part = pos_acc[...]
    for k in range(4):
        row_all[o, k : k + 1, :] = row_lse_part[:, 128 * k : 128 * k + 128]
        row_all[o, 4 + k : 5 + k, :] = pos_part[:, 128 * k : 128 * k + 128]

    def row_copy(k):
        other, dev = outer_peer(k)
        send = copy(row_all.at[o], row_all.at[o], row_ss.at[k], row_rs.at[o], dev)
        recv = copy(row_all.at[o], row_all.at[other], row_ss.at[k], row_rs.at[other], dev)
        return send, recv

    def row_start(k, _):
        row_copy(k)[0].start()
        return 0

    lax.fori_loop(1, NO, row_start, 0)
    sib_col.wait_recv()
    a0, a1 = col_part[...], col_sib[...]
    top = jnp.maximum(a0, a1)
    col_all[chip] = top + jnp.log(jnp.exp2(a0 - top) + jnp.exp2(a1 - top)) * (1.0 / LN2)

    def col_copy(k):
        other, dev = chip_peer(k)
        send = copy(col_all.at[chip], col_all.at[chip], col_ss.at[k], col_rs.at[chip], dev)
        recv = copy(col_all.at[chip], col_all.at[other], col_ss.at[k], col_rs.at[other], dev)
        return send, recv

    def col_start(k, _):
        by = lax.div(k, 2)
        col_copy(8 + jnp.where(lax.rem(k, 2) == 0, by, -by))[0].start()
        return 0

    lax.fori_loop(1, 16, col_start, 0)

    def row_wait(k, _):
        row_copy(k)[1].wait_recv()
        return 0

    lax.fori_loop(1, NO, row_wait, 0)
    rall = row_all[...]
    row_lse4 = lse_of(rall[:, 0:4, :], 0)[0]
    pos4 = jnp.sum(rall[:, 4:8, :], axis=0)
    for k in range(4):
        row_wide[:, 128 * k : 128 * k + 128] = row_lse4[k : k + 1, :] + 1.0
    sum_r[...] = jnp.broadcast_to(jnp.sum(row_lse4 - 2.0 * pos4, keepdims=True), (8, 128))
    sib_r = copy(sum_r, sum_r_sib, r1_ss.at[0], r1_rs.at[0], sib)
    sib_r.start()

    def col_wait(k, _):
        col_copy(k)[1].wait_recv()
        return 0

    lax.fori_loop(1, 16, col_wait, 0)
    col_lse = lse_of(col_all[...], 0)[0]
    for k in range(NZ):
        col_wide[k * GROUP : (k + 1) * GROUP, :] = jnp.broadcast_to(
            col_lse[k : k + 1, :] + 1.0, (128, GROUP)
        ).T
    def passage_set(oo):
        return lax.rem(lax.div(oo, 4) + xh, 2) * 4 + lax.rem(oo, 4)

    sum_c_all[passage_set(o)] = jnp.broadcast_to(jnp.sum(col_lse, keepdims=True), (8, 128))

    def c_copy(k):
        other, dev = outer_peer(k)
        me, it = passage_set(o), passage_set(other)
        send = copy(sum_c_all.at[me], sum_c_all.at[me], ca_ss.at[k], ca_rs.at[me], dev)
        recv = copy(sum_c_all.at[me], sum_c_all.at[it], ca_ss.at[k], ca_rs.at[it], dev)
        return send, recv

    def far(t):
        by = 4 - lax.div(t + 1, 2)
        return wrap(jnp.where(lax.rem(t, 2) == 1, by, -by))

    def weights_of(t):
        g = far(t)
        s = scores[rows(g, GROUP), :]
        cl = col_wide[rows(g, GROUP), :]
        w = jnp.exp2(s - row_wide[...]) + jnp.exp2(s - jnp.concatenate([cl] * 4, axis=1))
        weights[rows(g, GROUP), :] = (w - jnp.where(mask_of(g), 1.0, 0.0)).astype(BF16)

    def tile(t, _):
        weights_of(t)
        return 0

    def q_copy(st, other):
        dev = (b, other)
        i, mine_i = st * NO + other, st * NO + o
        send = copy(q_out.at[i], q_in.at[mine_i], q_ss.at[i], q_rs.at[mine_i], dev)
        recv = copy(q_out.at[i], q_in.at[i], q_ss.at[i], q_rs.at[i], dev)
        return send, recv

    def q_stage(st):
        g = dot(weights[:, st * 256 : (st + 1) * 256], pall[...], TN)
        for other in range(NO):
            part = g[other * HALF : (other + 1) * HALF, :]

            @pl.when(other == o)
            def _():
                q_own[st] = part

            @pl.when(other != o)
            def _():
                q_out[st * NO + other] = part.astype(BF16)
                q_copy(st, other)[0].start()

    def sib_copy(i):
        return copy(sib_out.at[i], sib_in.at[i], sib_ss.at[i], sib_rs.at[i], sib)

    def slot(way, d, xx):
        return way * 8 + (d - 1) * 2 + xx

    def ring_copy(way, d, xx, h):
        i = slot(way, d, xx)
        part = pl.ds(h * HALF, HALF)
        return copy(
            ring_out.at[i, part], ring_in.at[i, part],
            ring_ss.at[i * 2 + h], ring_rs.at[i * 2 + h], up if way == 0 else down,
        )

    def arrived(way, d, xx, h):
        ring_copy(way, d, xx, h).wait_recv()
        return ring_in[slot(way, d, xx), h * HALF : (h + 1) * HALF, :].astype(F32)

    def joined(dz, xx, h):
        i = wrap(dz) * 2 + xx
        if h == 0:
            sib_copy(i).wait_recv()
        part = slice(h * HALF, (h + 1) * HALF)
        return mine[i, part, :] + sib_in[i, part, :].astype(F32)

    def ring_send(d, xx_up, carry):
        for h in range(2):
            for way, xx in ((0, xx_up), (1, 1 - xx_up)):
                value = joined(d if way == 0 else -d, xx, h)
                if carry:
                    value = value + arrived(way, d + 1, xx, h)
                ring_out[slot(way, d, xx), h * HALF : (h + 1) * HALF, :] = value.astype(BF16)
                ring_copy(way, d, xx, h).start()

    def last_copy(way, rel, h):
        i = slot(way, 1, rel)
        part = pl.ds(h * HALF, HALF)
        to = at(wrap(1 if way == 0 else -1), xh if rel == 0 else 1 - xh, c)
        return copy(
            ring_out.at[i, part], ring_in.at[i, part],
            ring_ss.at[i * 2 + h], ring_rs.at[i * 2 + h], to,
        )

    def last_send(rel):
        xx = xh if rel == 0 else 1 - xh
        for h in range(2):
            part = slice(h * HALF, (h + 1) * HALF)
            for way in range(2):
                value = joined(1 if way == 0 else -1, xx, h) + arrived(way, 2, xx, h)
                ring_out[slot(way, 1, rel), part, :] = value.astype(BF16)
                last_copy(way, rel, h).start()

    def x_copy(h):
        part = pl.ds(h * HALF, HALF)
        return copy(x_out.at[part], x_in.at[part], x_ss.at[h], x_rs.at[h], x2)

    def second(t, _):
        pl.when(t < 2)(lambda: weights_of(t))

        @pl.when(t == 2)
        def _():
            lax.fori_loop(2, NZ, tile, 0)
            q_stage(0)

        zz = far(t)
        pres[...] = SHARP * dot(weights[rows(zz, GROUP), :], qh[...], NN)
        for xx in range(2):
            i = zz * 2 + xx
            sib_out[i] = pres[rows(xx * 2 + 1 - c), :].astype(BF16)
            sib_copy(i).start()
            mine[i] = pres[rows(xx * 2 + c), :]
        pl.when(t == 1)(lambda: ring_send(4, 0, False))
        pl.when(t == 3)(lambda: ring_send(3, 1, False))
        return 0

    lax.fori_loop(0, 8, second, 0)
    q_stage(1)
    ring_send(3, 0, True)
    for h in range(2):
        x_out[h * HALF : (h + 1) * HALF, :] = joined(0, 1 - xh, h).astype(BF16)
        x_copy(h).start()

    def c_start(k, _):
        c_copy(k)[0].start()
        return 0

    lax.fori_loop(1, NO, c_start, 0)
    sib_r.wait_recv()
    sum_r_all[chip] = sum_r[...] + sum_r_sib[...]

    def r_copy(k):
        other, dev = chip_peer(k)
        send = copy(sum_r_all.at[chip], sum_r_all.at[chip], ra_ss.at[k], ra_rs.at[chip], dev)
        recv = copy(sum_r_all.at[chip], sum_r_all.at[other], ra_ss.at[k], ra_rs.at[other], dev)
        return send, recv

    def r_start(k, _):
        r_copy(k)[0].start()
        return 0

    lax.fori_loop(1, 16, r_start, 0)

    def ag_done(k, _):
        ag_copy(b, 0, k, sib).wait_send()
        return 0

    def as_done(k, _):
        as_copy(b, k).wait_send()
        return 0

    def row_done(k, _):
        row_copy(k)[0].wait_send()
        return 0

    def col_done(k, _):
        col_copy(k)[0].wait_send()
        return 0

    lax.fori_loop(0, sent[0], ag_done, 0)
    lax.fori_loop(0, sent[1], as_done, 0)
    lax.fori_loop(1, NO, row_done, 0)
    lax.fori_loop(1, 16, col_done, 0)
    sib_col.wait_send()
    sib_r.wait_send()
    ring_send(2, 1, True)
    ring_send(2, 0, True)

    def sib_done(k, _):
        sib_copy(k).wait_send()
        return 0

    lax.fori_loop(0, 16, sib_done, 0)

    def q_rows(st, other):
        return pl.ds(pl.multiple_of(st * 256 + other * HALF, HALF), HALF)

    def f_copy(st, k):
        other, dev = outer_peer(k)
        here, there = q_fin.at[q_rows(st, o)], q_fin.at[q_rows(st, other)]
        send = copy(q_done_rows.at[st], here, f_ss.at[st * NO + k], f_rs.at[st * NO + o], dev)
        recv = copy(q_done_rows.at[st], there, f_ss.at[st * NO + k], f_rs.at[st * NO + other], dev)
        return send, recv

    def f_own(st):
        return pltpu.make_async_copy(q_done_rows.at[st], q_fin.at[q_rows(st, o)], own_sem.at[st])

    def q_finish(st):
        def q_add(k, _):
            other, _dev = outer_peer(k)
            q_copy(st, other)[1].wait_recv()
            q_own[st] += q_in[st * NO + other].astype(F32)
            return 0

        lax.fori_loop(1, NO, q_add, 0)
        qv = q_ref[q_rows(st, o), :]
        q_inv = lax.rsqrt(jnp.sum(qv * qv, axis=1, keepdims=True) + EPS)
        qu = qv * q_inv
        qg = SHARP * q_own[st]
        q_done_rows[st] = (
            q_inv * (qg - qu * jnp.sum(qu * qg, axis=1, keepdims=True))
        ).astype(BF16)

        def f_start(k, _):
            f_copy(st, k)[0].start()
            return 0

        lax.fori_loop(1, NO, f_start, 0)
        f_own(st).start()

    q_finish(0)
    last_send(1)
    last_send(0)
    for way in range(2):
        for d, xx in ((4, way), (3, 0), (3, 1)):
            for h in range(2):
                ring_copy(way, d, xx, h).wait_send()
    q_finish(1)

    def q_done(k, _):
        for st in range(2):
            q_copy(st, outer_peer(k)[0])[0].wait_send()
        return 0

    lax.fori_loop(1, NO, q_done, 0)

    own_i = z * 2 + xh

    def last_arrived(way, rel, h):
        last_copy(way, rel, h).wait_recv()
        return ring_in[slot(way, 1, rel), h * HALF : (h + 1) * HALF, :].astype(F32)

    def c_wait(k, _):
        c_copy(k)[1].wait_recv()
        return 0

    def r_wait(k, _):
        r_copy(k)[1].wait_recv()
        return 0

    lax.fori_loop(1, NO, c_wait, 0)
    lax.fori_loop(1, 16, r_wait, 0)
    loss_ref[...] = (jnp.sum(sum_r_all[...], axis=0) + jnp.sum(sum_c_all[...], axis=0)) * (
        LN2 / (2.0 * NB * NP * NO)
    )

    pu = p_ref[...]
    p_inv2 = lax.rsqrt(jnp.sum(pu * pu, axis=1, keepdims=True) + EPS)
    pu = pu * p_inv2

    for h in range(2):
        part = slice(h * HALF, (h + 1) * HALF)
        x_copy(h).wait_recv()
        g = joined(0, xh, h) + x_in[part, :].astype(F32)
        for rel in (1, 0):
            g = g + last_arrived(0, rel, h) + last_arrived(1, rel, h)
        u = pu[part, :]
        po_ref[part, :] = p_inv2[part, :] * (g - u * jnp.sum(u * g, axis=1, keepdims=True))

    def f_wait(k, _):
        f_copy(0, k)[1].wait_recv()
        f_copy(1, k)[1].wait_recv()
        return 0

    lax.fori_loop(1, NO, f_wait, 0)

    for h in range(2):
        x_copy(h).wait_send()

    def outer_done(k, _):
        c_copy(k)[0].wait_send()
        for st in range(2):
            f_copy(st, k)[0].wait_send()
        return 0

    lax.fori_loop(1, NO, outer_done, 0)

    def chip_done(k, _):
        r_copy(k)[0].wait_send()
        return 0

    lax.fori_loop(1, 16, chip_done, 0)
    for way in range(2):
        for d in (1, 2):
            for xx in range(2):
                for h in range(2):
                    ring_copy(way, d, xx, h).wait_send()
    for st in range(2):
        f_own(st).wait()


def widen(q_ref, p_ref, loss_ref, qo_ref, po_ref, lo_ref):
    qo_ref[...] = q_ref[...].astype(F32)
    po_ref[...] = p_ref[...]
    lo_ref[...] = loss_ref[0:1, 0:1]


def per_device(queries, passages, positive_id):
    vmem = pl.BlockSpec(memory_space=pltpu.VMEM)
    hbm = pl.BlockSpec(memory_space=pl.ANY)
    dma = pltpu.SemaphoreType.DMA
    scratch = [
        pltpu.VMEM((NQ, D), F32),
        pltpu.VMEM((NP, D), F32),
        pltpu.VMEM((1, NQ), jnp.int32),
        dma((3,)),
        pltpu.VMEM((NB * NP, D), BF16),
        pltpu.VMEM((NQ, D), BF16),
        pltpu.VMEM((NB * NP, NQ), F32),
        pltpu.VMEM((NB * NP, NQ), BF16),
        pltpu.VMEM((16, NP, D), F32),
        pltpu.VMEM((GROUP, D), F32),
        pltpu.VMEM((16, NP, D), BF16),
        pltpu.VMEM((16, NP, D), BF16),
        pltpu.VMEM((16, NP, D), BF16),
        pltpu.VMEM((16, NP, D), BF16),
        pltpu.VMEM((NP, D), BF16),
        pltpu.VMEM((NP, D), BF16),
        pltpu.VMEM((2 * NO, HALF, D), BF16),
        pltpu.VMEM((2 * NO, HALF, D), BF16),
        pltpu.VMEM((2, HALF, D), F32),
        pltpu.VMEM((2, HALF, D), BF16),
        dma((2,)),
        pltpu.VMEM((8, NQ), F32),
        pltpu.VMEM((1, NQ), F32),
        pltpu.VMEM((1, NQ), F32),
        pltpu.VMEM((NZ, GROUP), F32),
        pltpu.VMEM((NZ, GROUP), F32),
        pltpu.VMEM((NB * NP, 128), F32),
        pltpu.VMEM((16, NZ, GROUP), F32),
        pltpu.VMEM((NO, 8, 128), F32),
        pltpu.VMEM((8, 128), F32),
        pltpu.VMEM((8, 128), F32),
        pltpu.VMEM((16, 8, 128), F32),
        pltpu.VMEM((NO, 8, 128), F32),
        dma((64,)), dma((2 * NB,)), dma((16,)),
        dma((1,)), dma((1,)),
        dma((16,)), dma((16,)),
        dma((NO,)), dma((NO,)),
        dma((16,)), dma((16,)),
        dma((32,)), dma((32,)),
        dma((2,)), dma((2,)),
        dma((2 * NO,)), dma((2 * NO,)),
        dma((2 * NO,)), dma((2 * NO,)),
        dma((1,)), dma((1,)),
        dma((16,)), dma((16,)),
        dma((NO,)), dma((NO,)),
    ]
    qd, pd, loss = pl.pallas_call(
        kernel,
        out_shape=(
            jax.ShapeDtypeStruct((NQ, D), BF16),
            jax.ShapeDtypeStruct((NP, D), F32),
            jax.ShapeDtypeStruct((8, 128), F32),
        ),
        in_specs=[hbm, hbm, hbm],
        out_specs=(hbm, vmem, vmem),
        scratch_shapes=scratch,
        compiler_params=pltpu.CompilerParams(
            collective_id=0, has_side_effects=True, vmem_limit_bytes=56 * 2**20
        ),
    )(queries, passages, positive_id.reshape(1, NQ))
    parts = 2
    return pl.pallas_call(
        widen,
        grid=(parts,),
        out_shape=(
            jax.ShapeDtypeStruct((NQ, D), F32),
            jax.ShapeDtypeStruct((NP, D), F32),
            jax.ShapeDtypeStruct((1, 1), F32),
        ),
        in_specs=[
            pl.BlockSpec((NQ // parts, D), lambda i: (i, 0)),
            pl.BlockSpec((NP // parts, D), lambda i: (i, 0)),
            pl.BlockSpec((8, 128), lambda i: (0, 0)),
        ],
        out_specs=(
            pl.BlockSpec((NQ // parts, D), lambda i: (i, 0)),
            pl.BlockSpec((NP // parts, D), lambda i: (i, 0)),
            pl.BlockSpec((1, 1), lambda i: (0, 0)),
        ),
    )(qd, pd, loss)


def solution(mesh):
    def step(queries, passages, positive_id):
        qd, pd, loss = per_device(queries, passages, positive_id)
        return qd, pd, loss.reshape(())

    placed = (P("blk", None), P(("outer", "blk"), None), P("blk"))
    return jax.shard_map(
        step,
        mesh=mesh,
        in_specs=placed,
        out_specs=(P("blk", None), P(("outer", "blk"), None), P()),
        check_vma=False,
    )
```

```python
import jax
import jax.numpy as jnp
from jax import lax
from jax.experimental import pallas as pl
from jax.experimental.pallas import tpu as pltpu
from jax.sharding import PartitionSpec as P

MESH = pl.DeviceIdType.MESH
SHARP = 125.0
EPS = 1e-06
LN2 = 0.6931471805599453
SHARP2 = SHARP / LN2
HALF = 32
CROSS = (0,)
ORDER = (
    ((1, 0), (1, 1), (0, 1)), ((2, 0), (2, 1)), (), ((3, 0), (3, 1)), (), (), ((4, 0), (4, 1)), (),
)
D = 1024
NQ = 512
NP = 64
NB = 32
NO = 8
NZ = 8
GROUP = 4 * NP
F32 = jnp.float32
BF16 = jnp.bfloat16
NT = (((1,), (1,)), ((), ()))
NN = (((1,), (0,)), ((), ()))
TN = (((0,), (0,)), ((), ()))


def dot(a, b, dims):
    return lax.dot_general(a, b, dims, preferred_element_type=F32)


def lse_of(parts, axis):
    top = jnp.max(parts, axis=axis, keepdims=True)
    return top + jnp.log(jnp.sum(jnp.exp2(parts - top), axis=axis, keepdims=True)) * (1.0 / LN2)


def kernel(
    q_any, p_any, id_any,
    q_fin, po_ref, loss_ref,
    q_ref, p_ref, id_ref, in_sem,
    pall, qh, scores, weights, mine, pres, sib_out, sib_in, ring_out, ring_in,
    x_out, x_in, q_out, q_in, q_own, q_done_rows, own_sem,
    row_part, row_wide, pos_acc, col_part, col_sib, col_wide, col_all, row_all,
    sum_r, sum_r_sib, sum_r_all, sum_c_all,
    ag_ss, ag_rs, as_ss, cs_ss, cs_rs, col_ss, col_rs, row_ss, row_rs,
    sib_ss, sib_rs, ring_ss, ring_rs, x_ss, x_rs, q_ss, q_rs, f_ss, f_rs,
    r1_ss, r1_rs, ra_ss, ra_rs, ca_ss, ca_rs,
):
    b = lax.axis_index("blk")
    o = lax.axis_index("outer")
    c = lax.rem(b, 2)
    xh = lax.rem(lax.div(b, 2), 2)
    z = lax.div(b, 4)
    chip = z * 2 + xh

    def blk_of(zz, xx, cc):
        return (zz * 2 + xx) * 2 + cc

    def wrap(dz):
        return lax.rem(z + dz + 16, NZ)

    y = lax.rem(o, 4)
    xl = lax.div(o, 4)

    def outer_of(xx):
        return lax.rem(xl + xx + xh, 2) * 4 + y

    def at(zz, xx, cc):
        return (blk_of(zz, xx, cc), outer_of(xx))

    sib = at(z, xh, 1 - c)
    x2 = at(z, 1 - xh, c)
    up = at(wrap(1), xh, c)
    down = at(wrap(-1), xh, c)
    x2_up = at(wrap(1), 1 - xh, c)
    x2_down = at(wrap(-1), 1 - xh, c)

    def chip_peer(k):
        other = lax.rem(chip + k, 16)
        return other, (other * 2 + c, outer_of(lax.rem(other, 2)))

    def outer_peer(k):
        other = lax.rem(o + k, NO)
        return other, (b, other)

    def copy(src, dst, ss, rs, dev):
        return pltpu.make_async_remote_copy(
            src_ref=src, dst_ref=dst, send_sem=ss, recv_sem=rs, device_id=dev, device_id_type=MESH
        )

    p_load = pltpu.make_async_copy(p_any, p_ref, in_sem.at[0])
    q_load = pltpu.make_async_copy(q_any, q_ref, in_sem.at[1])
    id_load = pltpu.make_async_copy(id_any, id_ref, in_sem.at[2])
    p_load.start()
    barrier = pltpu.get_barrier_semaphore()
    for dev in (x2, up, down, x2_up, x2_down, sib):
        pl.semaphore_signal(barrier, inc=1, device_id=dev, device_id_type=MESH)

    def greet_outer(k, _):
        pl.semaphore_signal(barrier, inc=1, device_id=outer_peer(k)[1], device_id_type=MESH)
        return 0

    lax.fori_loop(1, NO, greet_outer, 0)
    q_load.start()
    id_load.start()

    def rows(i, n=NP):
        return pl.ds(pl.multiple_of(i * n, n), n)

    def shard(i):
        return pall.at[rows(i)]

    p_load.wait()
    pv = p_ref[...]
    p_inv = lax.rsqrt(jnp.sum(pv * pv, axis=1, keepdims=True) + EPS)
    pall[rows(b), :] = (pv * p_inv).astype(BF16)
    pl.semaphore_wait(barrier, 6 + NO - 1)

    def piece(i, h):
        return pall.at[pl.ds(pl.multiple_of(i * NP + h * HALF, HALF), HALF)]

    def ag_copy(i, h, k, dev):
        return copy(piece(i, h), piece(i, h), ag_ss.at[k], ag_rs.at[i * 2 + h], dev)

    def as_copy(i, k):
        return copy(shard(i), shard(i), as_ss.at[k], ag_rs.at[i * 2], sib)

    sent = [0, 0]

    def pass_on(i, h, *devs):
        for dev in devs:
            ag_copy(i, h, sent[0], dev).start()
            sent[0] += 1

    def to_sib(i):
        as_copy(i, sent[1]).start()
        sent[1] += 1

    for h in range(2):
        pass_on(b, h, up, down, x2_up, x2_down)
    for h in range(2):
        pass_on(b, h, x2)
    to_sib(b)

    def norm_q(i, _):
        v = q_ref[rows(i), :]
        inv = lax.rsqrt(jnp.sum(v * v, axis=1, keepdims=True) + EPS)
        qh[rows(i), :] = (v * inv).astype(BF16)
        return 0

    q_load.wait()
    lax.fori_loop(0, NQ // NP, norm_q, 0)
    id_load.wait()
    pos_acc[...] = jnp.zeros_like(pos_acc)

    def own(dz, xrel):
        return blk_of(wrap(dz), xh if xrel == 0 else 1 - xh, c)

    sign = 2 * xh - 1

    def got(dz, xrel):
        sides = (dz,) if dz in (0, 4) else (-dz, dz)
        for h in range(2):
            for d in sides:
                i = own(d, xrel)
                ag_copy(i, h, 0, sib).wait_recv()
                if xrel == 0 and dz in CROSS and dz > 0:
                    pass_on(i, h, x2)
                if 0 < dz < 3 and (xrel == 0 or dz + 1 not in CROSS):
                    if d <= 0:
                        pass_on(i, h, up)
                    if d >= 0:
                        pass_on(i, h, down)
            if dz == 3 and (xrel == 0 or 4 not in CROSS):
                s = sign if xrel == 0 else -sign
                pass_on(
                    blk_of(wrap(3 * s), xh if xrel == 0 else 1 - xh, c), h, at(wrap(-s), xh, c)
                )
        for d in sides:
            to_sib(own(d, xrel))

    def from_sib(dz):
        for xx in range(2):
            as_copy(blk_of(wrap(dz), xx, 1 - c), 0).wait_recv()

    def gather_turn(t):
        for k, step in enumerate(ORDER):
            if t == k:
                for dz, xrel in step:
                    got(dz, xrel)
        from_sib((0, -1, 1, -2, 2, -3, 3, 4)[t])

    base = [outer_of(xx) * (NB * NP) for xx in range(2)]

    def mask_of(zz):
        row = lax.broadcasted_iota(jnp.int32, (GROUP, NQ), 0)
        return row + zz * GROUP + jnp.where(row < GROUP // 2, base[0], base[1]) == id_ref[...]

    def first(t, _):
        for k in range(8):
            pl.when(t == k)(lambda k=k: gather_turn(k))
        far_by = lax.div(t + 1, 2)
        zz = wrap(jnp.where(lax.rem(t, 2) == 1, -far_by, far_by))
        pg = pall[rows(zz, GROUP), :]
        s = SHARP2 * dot(pg, qh[...], NT)
        scores[rows(zz, GROUP), :] = s
        row_part[pl.ds(t, 1), :] = lse_of(s, 0)
        pos_acc[...] += jnp.sum(jnp.where(mask_of(zz), s, 0.0), axis=0, keepdims=True)
        st = SHARP2 * dot(qh[...], pg, NT)
        col_part[pl.ds(zz, 1), :] = lse_of(st, 0)
        return 0

    lax.fori_loop(0, 8, first, 0)

    sib_col = copy(col_part, col_sib, cs_ss.at[0], cs_rs.at[0], sib)
    sib_col.start()
    row_lse_part = lse_of(row_part[...], 0)
    pos_part = pos_acc[...]
    for k in range(4):
        row_all[o, k : k + 1, :] = row_lse_part[:, 128 * k : 128 * k + 128]
        row_all[o, 4 + k : 5 + k, :] = pos_part[:, 128 * k : 128 * k + 128]

    def row_copy(k):
        other, dev = outer_peer(k)
        send = copy(row_all.at[o], row_all.at[o], row_ss.at[k], row_rs.at[o], dev)
        recv = copy(row_all.at[o], row_all.at[other], row_ss.at[k], row_rs.at[other], dev)
        return send, recv

    def row_start(k, _):
        row_copy(k)[0].start()
        return 0

    lax.fori_loop(1, NO, row_start, 0)
    sib_col.wait_recv()
    a0, a1 = col_part[...], col_sib[...]
    top = jnp.maximum(a0, a1)
    col_all[chip] = top + jnp.log(jnp.exp2(a0 - top) + jnp.exp2(a1 - top)) * (1.0 / LN2)

    def col_copy(k):
        other, dev = chip_peer(k)
        send = copy(col_all.at[chip], col_all.at[chip], col_ss.at[k], col_rs.at[chip], dev)
        recv = copy(col_all.at[chip], col_all.at[other], col_ss.at[k], col_rs.at[other], dev)
        return send, recv

    def col_start(k, _):
        by = lax.div(k, 2)
        col_copy(8 + jnp.where(lax.rem(k, 2) == 0, by, -by))[0].start()
        return 0

    lax.fori_loop(1, 16, col_start, 0)

    def row_wait(k, _):
        row_copy(k)[1].wait_recv()
        return 0

    lax.fori_loop(1, NO, row_wait, 0)
    rall = row_all[...]
    row_lse4 = lse_of(rall[:, 0:4, :], 0)[0]
    pos4 = jnp.sum(rall[:, 4:8, :], axis=0)
    for k in range(4):
        row_wide[:, 128 * k : 128 * k + 128] = row_lse4[k : k + 1, :] + 1.0
    sum_r[...] = jnp.broadcast_to(jnp.sum(row_lse4 - 2.0 * pos4, keepdims=True), (8, 128))
    sib_r = copy(sum_r, sum_r_sib, r1_ss.at[0], r1_rs.at[0], sib)
    sib_r.start()

    def col_wait(k, _):
        col_copy(k)[1].wait_recv()
        return 0

    lax.fori_loop(1, 16, col_wait, 0)
    col_lse = lse_of(col_all[...], 0)[0]
    for k in range(NZ):
        col_wide[k * GROUP : (k + 1) * GROUP, :] = jnp.broadcast_to(
            col_lse[k : k + 1, :] + 1.0, (128, GROUP)
        ).T
    def passage_set(oo):
        return lax.rem(lax.div(oo, 4) + xh, 2) * 4 + lax.rem(oo, 4)

    sum_c_all[passage_set(o)] = jnp.broadcast_to(jnp.sum(col_lse, keepdims=True), (8, 128))

    def c_copy(k):
        other, dev = outer_peer(k)
        me, it = passage_set(o), passage_set(other)
        send = copy(sum_c_all.at[me], sum_c_all.at[me], ca_ss.at[k], ca_rs.at[me], dev)
        recv = copy(sum_c_all.at[me], sum_c_all.at[it], ca_ss.at[k], ca_rs.at[it], dev)
        return send, recv

    def far(t):
        by = 4 - lax.div(t + 1, 2)
        return wrap(jnp.where(lax.rem(t, 2) == 1, by, -by))

    def weights_of(t):
        g = far(t)
        s = scores[rows(g, GROUP), :]
        cl = col_wide[rows(g, GROUP), :]
        w = jnp.exp2(s - row_wide[...]) + jnp.exp2(s - jnp.concatenate([cl] * 4, axis=1))
        weights[rows(g, GROUP), :] = (w - jnp.where(mask_of(g), 1.0, 0.0)).astype(BF16)

    def tile(t, _):
        weights_of(t)
        return 0

    def q_copy(st, other):
        dev = (b, other)
        i, mine_i = st * NO + other, st * NO + o
        send = copy(q_out.at[i], q_in.at[mine_i], q_ss.at[i], q_rs.at[mine_i], dev)
        recv = copy(q_out.at[i], q_in.at[i], q_ss.at[i], q_rs.at[i], dev)
        return send, recv

    def q_stage(st):
        g = dot(weights[:, st * 256 : (st + 1) * 256], pall[...], TN)
        for other in range(NO):
            part = g[other * HALF : (other + 1) * HALF, :]

            @pl.when(other == o)
            def _():
                q_own[st] = part

            @pl.when(other != o)
            def _():
                q_out[st * NO + other] = part.astype(BF16)
                q_copy(st, other)[0].start()

    def sib_copy(i):
        return copy(sib_out.at[i], sib_in.at[i], sib_ss.at[i], sib_rs.at[i], sib)

    def slot(way, d, xx):
        return way * 8 + (d - 1) * 2 + xx

    def ring_copy(way, d, xx, h):
        i = slot(way, d, xx)
        part = pl.ds(h * HALF, HALF)
        return copy(
            ring_out.at[i, part], ring_in.at[i, part],
            ring_ss.at[i * 2 + h], ring_rs.at[i * 2 + h], up if way == 0 else down,
        )

    def arrived(way, d, xx, h):
        ring_copy(way, d, xx, h).wait_recv()
        return ring_in[slot(way, d, xx), h * HALF : (h + 1) * HALF, :].astype(F32)

    def joined(dz, xx, h):
        i = wrap(dz) * 2 + xx
        if h == 0:
            sib_copy(i).wait_recv()
        part = slice(h * HALF, (h + 1) * HALF)
        return mine[i, part, :] + sib_in[i, part, :].astype(F32)

    def ring_send(d, xx_up, carry):
        for h in range(2):
            for way, xx in ((0, xx_up), (1, 1 - xx_up)):
                value = joined(d if way == 0 else -d, xx, h)
                if carry:
                    value = value + arrived(way, d + 1, xx, h)
                ring_out[slot(way, d, xx), h * HALF : (h + 1) * HALF, :] = value.astype(BF16)
                ring_copy(way, d, xx, h).start()

    def last_copy(way, rel, h):
        i = slot(way, 1, rel)
        part = pl.ds(h * HALF, HALF)
        to = at(wrap(1 if way == 0 else -1), xh if rel == 0 else 1 - xh, c)
        return copy(
            ring_out.at[i, part], ring_in.at[i, part],
            ring_ss.at[i * 2 + h], ring_rs.at[i * 2 + h], to,
        )

    def last_send(rel):
        xx = xh if rel == 0 else 1 - xh
        for h in range(2):
            part = slice(h * HALF, (h + 1) * HALF)
            for way in range(2):
                value = joined(1 if way == 0 else -1, xx, h) + arrived(way, 2, xx, h)
                ring_out[slot(way, 1, rel), part, :] = value.astype(BF16)
                last_copy(way, rel, h).start()

    def x_copy(h):
        part = pl.ds(h * HALF, HALF)
        return copy(x_out.at[part], x_in.at[part], x_ss.at[h], x_rs.at[h], x2)

    def second(t, _):
        pl.when(t < 2)(lambda: weights_of(t))

        @pl.when(t == 2)
        def _():
            lax.fori_loop(2, NZ, tile, 0)
            q_stage(0)

        zz = far(t)
        pres[...] = SHARP * dot(weights[rows(zz, GROUP), :], qh[...], NN)
        for xx in range(2):
            i = zz * 2 + xx
            sib_out[i] = pres[rows(xx * 2 + 1 - c), :].astype(BF16)
            sib_copy(i).start()
            mine[i] = pres[rows(xx * 2 + c), :]
        pl.when(t == 1)(lambda: ring_send(4, 0, False))
        pl.when(t == 3)(lambda: ring_send(3, 1, False))
        return 0

    lax.fori_loop(0, 8, second, 0)
    q_stage(1)
    ring_send(3, 0, True)
    for h in range(2):
        x_out[h * HALF : (h + 1) * HALF, :] = joined(0, 1 - xh, h).astype(BF16)
        x_copy(h).start()

    def c_start(k, _):
        c_copy(k)[0].start()
        return 0

    lax.fori_loop(1, NO, c_start, 0)
    sib_r.wait_recv()
    sum_r_all[chip] = sum_r[...] + sum_r_sib[...]

    def r_copy(k):
        other, dev = chip_peer(k)
        send = copy(sum_r_all.at[chip], sum_r_all.at[chip], ra_ss.at[k], ra_rs.at[chip], dev)
        recv = copy(sum_r_all.at[chip], sum_r_all.at[other], ra_ss.at[k], ra_rs.at[other], dev)
        return send, recv

    def r_start(k, _):
        r_copy(k)[0].start()
        return 0

    lax.fori_loop(1, 16, r_start, 0)

    def ag_done(k, _):
        ag_copy(b, 0, k, sib).wait_send()
        return 0

    def as_done(k, _):
        as_copy(b, k).wait_send()
        return 0

    def row_done(k, _):
        row_copy(k)[0].wait_send()
        return 0

    def col_done(k, _):
        col_copy(k)[0].wait_send()
        return 0

    lax.fori_loop(0, sent[0], ag_done, 0)
    lax.fori_loop(0, sent[1], as_done, 0)
    lax.fori_loop(1, NO, row_done, 0)
    lax.fori_loop(1, 16, col_done, 0)
    sib_col.wait_send()
    sib_r.wait_send()
    ring_send(2, 1, True)
    ring_send(2, 0, True)

    def sib_done(k, _):
        sib_copy(k).wait_send()
        return 0

    lax.fori_loop(0, 16, sib_done, 0)

    def q_rows(st, other):
        return pl.ds(pl.multiple_of(st * 256 + other * HALF, HALF), HALF)

    def f_copy(st, k):
        other, dev = outer_peer(k)
        here, there = q_fin.at[q_rows(st, o)], q_fin.at[q_rows(st, other)]
        send = copy(q_done_rows.at[st], here, f_ss.at[st * NO + k], f_rs.at[st * NO + o], dev)
        recv = copy(q_done_rows.at[st], there, f_ss.at[st * NO + k], f_rs.at[st * NO + other], dev)
        return send, recv

    def f_own(st):
        return pltpu.make_async_copy(q_done_rows.at[st], q_fin.at[q_rows(st, o)], own_sem.at[st])

    def q_finish(st):
        def q_add(k, _):
            other, _dev = outer_peer(k)
            q_copy(st, other)[1].wait_recv()
            q_own[st] += q_in[st * NO + other].astype(F32)
            return 0

        lax.fori_loop(1, NO, q_add, 0)
        qv = q_ref[q_rows(st, o), :]
        q_inv = lax.rsqrt(jnp.sum(qv * qv, axis=1, keepdims=True) + EPS)
        qu = qv * q_inv
        qg = SHARP * q_own[st]
        q_done_rows[st] = (
            q_inv * (qg - qu * jnp.sum(qu * qg, axis=1, keepdims=True))
        ).astype(BF16)

        def f_start(k, _):
            f_copy(st, k)[0].start()
            return 0

        lax.fori_loop(1, NO, f_start, 0)
        f_own(st).start()

    q_finish(0)
    last_send(1)
    last_send(0)
    for way in range(2):
        for d, xx in ((4, way), (3, 0), (3, 1)):
            for h in range(2):
                ring_copy(way, d, xx, h).wait_send()
    q_finish(1)

    def q_done(k, _):
        for st in range(2):
            q_copy(st, outer_peer(k)[0])[0].wait_send()
        return 0

    lax.fori_loop(1, NO, q_done, 0)

    own_i = z * 2 + xh

    def last_arrived(way, rel, h):
        last_copy(way, rel, h).wait_recv()
        return ring_in[slot(way, 1, rel), h * HALF : (h + 1) * HALF, :].astype(F32)

    def c_wait(k, _):
        c_copy(k)[1].wait_recv()
        return 0

    def r_wait(k, _):
        r_copy(k)[1].wait_recv()
        return 0

    lax.fori_loop(1, NO, c_wait, 0)
    lax.fori_loop(1, 16, r_wait, 0)
    loss_ref[...] = (jnp.sum(sum_r_all[...], axis=0) + jnp.sum(sum_c_all[...], axis=0)) * (
        LN2 / (2.0 * NB * NP * NO)
    )

    pu = p_ref[...]
    p_inv2 = lax.rsqrt(jnp.sum(pu * pu, axis=1, keepdims=True) + EPS)
    pu = pu * p_inv2

    for h in range(2):
        part = slice(h * HALF, (h + 1) * HALF)
        x_copy(h).wait_recv()
        g = joined(0, xh, h) + x_in[part, :].astype(F32)
        for rel in (1, 0):
            g = g + last_arrived(0, rel, h) + last_arrived(1, rel, h)
        u = pu[part, :]
        po_ref[part, :] = p_inv2[part, :] * (g - u * jnp.sum(u * g, axis=1, keepdims=True))

    def f_wait(k, _):
        f_copy(0, k)[1].wait_recv()
        f_copy(1, k)[1].wait_recv()
        return 0

    lax.fori_loop(1, NO, f_wait, 0)

    for h in range(2):
        x_copy(h).wait_send()

    def outer_done(k, _):
        c_copy(k)[0].wait_send()
        for st in range(2):
            f_copy(st, k)[0].wait_send()
        return 0

    lax.fori_loop(1, NO, outer_done, 0)

    def chip_done(k, _):
        r_copy(k)[0].wait_send()
        return 0

    lax.fori_loop(1, 16, chip_done, 0)
    for way in range(2):
        for d in (1, 2):
            for xx in range(2):
                for h in range(2):
                    ring_copy(way, d, xx, h).wait_send()
    for st in range(2):
        f_own(st).wait()


def widen(q_ref, p_ref, loss_ref, qo_ref, po_ref, lo_ref):
    qo_ref[...] = q_ref[...].astype(F32)
    po_ref[...] = p_ref[...]
    lo_ref[...] = loss_ref[0:1, 0:1]


def per_device(queries, passages, positive_id):
    vmem = pl.BlockSpec(memory_space=pltpu.VMEM)
    hbm = pl.BlockSpec(memory_space=pl.ANY)
    dma = pltpu.SemaphoreType.DMA
    scratch = [
        pltpu.VMEM((NQ, D), F32),
        pltpu.VMEM((NP, D), F32),
        pltpu.VMEM((1, NQ), jnp.int32),
        dma((3,)),
        pltpu.VMEM((NB * NP, D), BF16),
        pltpu.VMEM((NQ, D), BF16),
        pltpu.VMEM((NB * NP, NQ), F32),
        pltpu.VMEM((NB * NP, NQ), BF16),
        pltpu.VMEM((16, NP, D), F32),
        pltpu.VMEM((GROUP, D), F32),
        pltpu.VMEM((16, NP, D), BF16),
        pltpu.VMEM((16, NP, D), BF16),
        pltpu.VMEM((16, NP, D), BF16),
        pltpu.VMEM((16, NP, D), BF16),
        pltpu.VMEM((NP, D), BF16),
        pltpu.VMEM((NP, D), BF16),
        pltpu.VMEM((2 * NO, HALF, D), BF16),
        pltpu.VMEM((2 * NO, HALF, D), BF16),
        pltpu.VMEM((2, HALF, D), F32),
        pltpu.VMEM((2, HALF, D), BF16),
        dma((2,)),
        pltpu.VMEM((8, NQ), F32),
        pltpu.VMEM((1, NQ), F32),
        pltpu.VMEM((1, NQ), F32),
        pltpu.VMEM((NZ, GROUP), F32),
        pltpu.VMEM((NZ, GROUP), F32),
        pltpu.VMEM((NB * NP, 128), F32),
        pltpu.VMEM((16, NZ, GROUP), F32),
        pltpu.VMEM((NO, 8, 128), F32),
        pltpu.VMEM((8, 128), F32),
        pltpu.VMEM((8, 128), F32),
        pltpu.VMEM((16, 8, 128), F32),
        pltpu.VMEM((NO, 8, 128), F32),
        dma((64,)), dma((2 * NB,)), dma((16,)),
        dma((1,)), dma((1,)),
        dma((16,)), dma((16,)),
        dma((NO,)), dma((NO,)),
        dma((16,)), dma((16,)),
        dma((32,)), dma((32,)),
        dma((2,)), dma((2,)),
        dma((2 * NO,)), dma((2 * NO,)),
        dma((2 * NO,)), dma((2 * NO,)),
        dma((1,)), dma((1,)),
        dma((16,)), dma((16,)),
        dma((NO,)), dma((NO,)),
    ]
    qd, pd, loss = pl.pallas_call(
        kernel,
        out_shape=(
            jax.ShapeDtypeStruct((NQ, D), BF16),
            jax.ShapeDtypeStruct((NP, D), F32),
            jax.ShapeDtypeStruct((8, 128), F32),
        ),
        in_specs=[hbm, hbm, hbm],
        out_specs=(hbm, vmem, vmem),
        scratch_shapes=scratch,
        compiler_params=pltpu.CompilerParams(
            collective_id=0, has_side_effects=True, vmem_limit_bytes=56 * 2**20
        ),
    )(queries, passages, positive_id.reshape(1, NQ))
    parts = 2
    return pl.pallas_call(
        widen,
        grid=(parts,),
        out_shape=(
            jax.ShapeDtypeStruct((NQ, D), F32),
            jax.ShapeDtypeStruct((NP, D), F32),
            jax.ShapeDtypeStruct((1, 1), F32),
        ),
        in_specs=[
            pl.BlockSpec((NQ // parts, D), lambda i: (i, 0)),
            pl.BlockSpec((NP // parts, D), lambda i: (i, 0)),
            pl.BlockSpec((8, 128), lambda i: (0, 0)),
        ],
        out_specs=(
            pl.BlockSpec((NQ // parts, D), lambda i: (i, 0)),
            pl.BlockSpec((NP // parts, D), lambda i: (i, 0)),
            pl.BlockSpec((1, 1), lambda i: (0, 0)),
        ),
    )(qd, pd, loss)


def solution(mesh):
    def step(queries, passages, positive_id):
        qd, pd, loss = per_device(queries, passages, positive_id)
        return qd, pd, loss.reshape(())

    placed = (P("blk", None), P(("outer", "blk"), None), P("blk"))
    return jax.shard_map(
        step,
        mesh=mesh,
        in_specs=placed,
        out_specs=(P("blk", None), P(("outer", "blk"), None), P()),
        check_vma=False,
    )
```

```python
import jax
import jax.numpy as jnp
from jax import lax
from jax.experimental import pallas as pl
from jax.experimental.pallas import tpu as pltpu
from jax.sharding import PartitionSpec as P

MESH = pl.DeviceIdType.MESH
SHARP = 125.0
EPS = 1e-06
LN2 = 0.6931471805599453
SHARP2 = SHARP / LN2
HALF = 32
CROSS = (0,)
ORDER = (
    ((1, 0), (1, 1), (0, 1)), ((2, 0), (2, 1)), (), ((3, 0), (3, 1)), (), (), ((4, 0), (4, 1)), (),
)
D = 1024
NQ = 512
NP = 64
NB = 32
NO = 8
NZ = 8
GROUP = 4 * NP
F32 = jnp.float32
BF16 = jnp.bfloat16
NT = (((1,), (1,)), ((), ()))
NN = (((1,), (0,)), ((), ()))
TN = (((0,), (0,)), ((), ()))


def dot(a, b, dims):
    return lax.dot_general(a, b, dims, preferred_element_type=F32)


def lse_of(parts, axis):
    top = jnp.max(parts, axis=axis, keepdims=True)
    return top + jnp.log(jnp.sum(jnp.exp2(parts - top), axis=axis, keepdims=True)) * (1.0 / LN2)


def kernel(
    q_any, p_any, id_any,
    q_fin, po_ref, loss_ref,
    q_ref, p_ref, id_ref, in_sem,
    pall, qh, scores, weights, mine, pres, sib_out, sib_in, ring_out, ring_in,
    x_out, x_in, q_out, q_in, q_own, q_done_rows, own_sem,
    row_part, row_wide, pos_acc, col_part, col_sib, col_wide, col_all, row_all,
    sum_r, sum_r_sib, sum_r_all, sum_c_all,
    ag_ss, ag_rs, as_ss, cs_ss, cs_rs, col_ss, col_rs, row_ss, row_rs,
    sib_ss, sib_rs, ring_ss, ring_rs, x_ss, x_rs, q_ss, q_rs, f_ss, f_rs,
    r1_ss, r1_rs, ra_ss, ra_rs, ca_ss, ca_rs,
):
    b = lax.axis_index("blk")
    o = lax.axis_index("outer")
    c = lax.rem(b, 2)
    xh = lax.rem(lax.div(b, 2), 2)
    z = lax.div(b, 4)
    chip = z * 2 + xh

    def blk_of(zz, xx, cc):
        return (zz * 2 + xx) * 2 + cc

    def wrap(dz):
        return lax.rem(z + dz + 16, NZ)

    y = lax.rem(o, 4)
    xl = lax.div(o, 4)

    def outer_of(xx):
        return lax.rem(xl + xx + xh, 2) * 4 + y

    def at(zz, xx, cc):
        return (blk_of(zz, xx, cc), outer_of(xx))

    sib = at(z, xh, 1 - c)
    x2 = at(z, 1 - xh, c)
    up = at(wrap(1), xh, c)
    down = at(wrap(-1), xh, c)
    x2_up = at(wrap(1), 1 - xh, c)
    x2_down = at(wrap(-1), 1 - xh, c)

    def chip_peer(k):
        other = lax.rem(chip + k, 16)
        return other, (other * 2 + c, outer_of(lax.rem(other, 2)))

    def outer_peer(k):
        other = lax.rem(o + k, NO)
        return other, (b, other)

    def copy(src, dst, ss, rs, dev):
        return pltpu.make_async_remote_copy(
            src_ref=src, dst_ref=dst, send_sem=ss, recv_sem=rs, device_id=dev, device_id_type=MESH
        )

    p_load = pltpu.make_async_copy(p_any, p_ref, in_sem.at[0])
    q_load = pltpu.make_async_copy(q_any, q_ref, in_sem.at[1])
    id_load = pltpu.make_async_copy(id_any, id_ref, in_sem.at[2])
    p_load.start()
    barrier = pltpu.get_barrier_semaphore()
    for dev in (x2, up, down, x2_up, x2_down, sib):
        pl.semaphore_signal(barrier, inc=1, device_id=dev, device_id_type=MESH)

    def greet_outer(k, _):
        pl.semaphore_signal(barrier, inc=1, device_id=outer_peer(k)[1], device_id_type=MESH)
        return 0

    lax.fori_loop(1, NO, greet_outer, 0)
    q_load.start()
    id_load.start()

    def rows(i, n=NP):
        return pl.ds(pl.multiple_of(i * n, n), n)

    def shard(i):
        return pall.at[rows(i)]

    p_load.wait()
    pv = p_ref[...]
    p_inv = lax.rsqrt(jnp.sum(pv * pv, axis=1, keepdims=True) + EPS)
    pall[rows(b), :] = (pv * p_inv).astype(BF16)
    pl.semaphore_wait(barrier, 6 + NO - 1)

    def piece(i, h):
        return pall.at[pl.ds(pl.multiple_of(i * NP + h * HALF, HALF), HALF)]

    def ag_copy(i, h, k, dev):
        return copy(piece(i, h), piece(i, h), ag_ss.at[k], ag_rs.at[i * 2 + h], dev)

    def as_copy(i, k):
        return copy(shard(i), shard(i), as_ss.at[k], ag_rs.at[i * 2], sib)

    sent = [0, 0]

    def pass_on(i, h, *devs):
        for dev in devs:
            ag_copy(i, h, sent[0], dev).start()
            sent[0] += 1

    def to_sib(i):
        as_copy(i, sent[1]).start()
        sent[1] += 1

    for h in range(2):
        pass_on(b, h, up, down, x2_up, x2_down)
    for h in range(2):
        pass_on(b, h, x2)
    to_sib(b)

    def norm_q(i, _):
        v = q_ref[rows(i), :]
        inv = lax.rsqrt(jnp.sum(v * v, axis=1, keepdims=True) + EPS)
        qh[rows(i), :] = (v * inv).astype(BF16)
        return 0

    q_load.wait()
    lax.fori_loop(0, NQ // NP, norm_q, 0)
    id_load.wait()
    pos_acc[...] = jnp.zeros_like(pos_acc)

    def own(dz, xrel):
        return blk_of(wrap(dz), xh if xrel == 0 else 1 - xh, c)

    sign = 2 * xh - 1

    def got(dz, xrel):
        sides = (dz,) if dz in (0, 4) else (-dz, dz)
        for h in range(2):
            for d in sides:
                i = own(d, xrel)
                ag_copy(i, h, 0, sib).wait_recv()
                if xrel == 0 and dz in CROSS and dz > 0:
                    pass_on(i, h, x2)
                if 0 < dz < 3 and (xrel == 0 or dz + 1 not in CROSS):
                    if d <= 0:
                        pass_on(i, h, up)
                    if d >= 0:
                        pass_on(i, h, down)
            if dz == 3 and (xrel == 0 or 4 not in CROSS):
                s = sign if xrel == 0 else -sign
                pass_on(
                    blk_of(wrap(3 * s), xh if xrel == 0 else 1 - xh, c), h, at(wrap(-s), xh, c)
                )
        for d in sides:
            to_sib(own(d, xrel))

    def from_sib(dz):
        for xx in range(2):
            as_copy(blk_of(wrap(dz), xx, 1 - c), 0).wait_recv()

    def gather_turn(t):
        for k, step in enumerate(ORDER):
            if t == k:
                for dz, xrel in step:
                    got(dz, xrel)
        from_sib((0, -1, 1, -2, 2, -3, 3, 4)[t])

    base = [outer_of(xx) * (NB * NP) for xx in range(2)]

    def mask_of(zz):
        row = lax.broadcasted_iota(jnp.int32, (GROUP, NQ), 0)
        return row + zz * GROUP + jnp.where(row < GROUP // 2, base[0], base[1]) == id_ref[...]

    def first(t, _):
        for k in range(8):
            pl.when(t == k)(lambda k=k: gather_turn(k))
        far_by = lax.div(t + 1, 2)
        zz = wrap(jnp.where(lax.rem(t, 2) == 1, -far_by, far_by))
        pg = pall[rows(zz, GROUP), :]
        s = SHARP2 * dot(pg, qh[...], NT)
        scores[rows(zz, GROUP), :] = s
        row_part[pl.ds(t, 1), :] = lse_of(s, 0)
        pos_acc[...] += jnp.sum(jnp.where(mask_of(zz), s, 0.0), axis=0, keepdims=True)
        st = SHARP2 * dot(qh[...], pg, NT)
        col_part[pl.ds(zz, 1), :] = lse_of(st, 0)
        return 0

    lax.fori_loop(0, 8, first, 0)

    sib_col = copy(col_part, col_sib, cs_ss.at[0], cs_rs.at[0], sib)
    sib_col.start()
    row_lse_part = lse_of(row_part[...], 0)
    pos_part = pos_acc[...]
    for k in range(4):
        row_all[o, k : k + 1, :] = row_lse_part[:, 128 * k : 128 * k + 128]
        row_all[o, 4 + k : 5 + k, :] = pos_part[:, 128 * k : 128 * k + 128]

    def row_copy(k):
        other, dev = outer_peer(k)
        send = copy(row_all.at[o], row_all.at[o], row_ss.at[k], row_rs.at[o], dev)
        recv = copy(row_all.at[o], row_all.at[other], row_ss.at[k], row_rs.at[other], dev)
        return send, recv

    def row_start(k, _):
        row_copy(k)[0].start()
        return 0

    lax.fori_loop(1, NO, row_start, 0)
    sib_col.wait_recv()
    a0, a1 = col_part[...], col_sib[...]
    top = jnp.maximum(a0, a1)
    col_all[chip] = top + jnp.log(jnp.exp2(a0 - top) + jnp.exp2(a1 - top)) * (1.0 / LN2)

    def col_copy(k):
        other, dev = chip_peer(k)
        send = copy(col_all.at[chip], col_all.at[chip], col_ss.at[k], col_rs.at[chip], dev)
        recv = copy(col_all.at[chip], col_all.at[other], col_ss.at[k], col_rs.at[other], dev)
        return send, recv

    def col_start(k, _):
        by = lax.div(k, 2)
        col_copy(8 + jnp.where(lax.rem(k, 2) == 0, by, -by))[0].start()
        return 0

    lax.fori_loop(1, 16, col_start, 0)

    def row_wait(k, _):
        row_copy(k)[1].wait_recv()
        return 0

    lax.fori_loop(1, NO, row_wait, 0)
    rall = row_all[...]
    row_lse4 = lse_of(rall[:, 0:4, :], 0)[0]
    pos4 = jnp.sum(rall[:, 4:8, :], axis=0)
    for k in range(4):
        row_wide[:, 128 * k : 128 * k + 128] = row_lse4[k : k + 1, :] + 1.0
    sum_r[...] = jnp.broadcast_to(jnp.sum(row_lse4 - 2.0 * pos4, keepdims=True), (8, 128))
    sib_r = copy(sum_r, sum_r_sib, r1_ss.at[0], r1_rs.at[0], sib)
    sib_r.start()

    def col_wait(k, _):
        col_copy(k)[1].wait_recv()
        return 0

    lax.fori_loop(1, 16, col_wait, 0)
    col_lse = lse_of(col_all[...], 0)[0]
    for k in range(NZ):
        col_wide[k * GROUP : (k + 1) * GROUP, :] = jnp.broadcast_to(
            col_lse[k : k + 1, :] + 1.0, (128, GROUP)
        ).T
    def passage_set(oo):
        return lax.rem(lax.div(oo, 4) + xh, 2) * 4 + lax.rem(oo, 4)

    sum_c_all[passage_set(o)] = jnp.broadcast_to(jnp.sum(col_lse, keepdims=True), (8, 128))

    def c_copy(k):
        other, dev = outer_peer(k)
        me, it = passage_set(o), passage_set(other)
        send = copy(sum_c_all.at[me], sum_c_all.at[me], ca_ss.at[k], ca_rs.at[me], dev)
        recv = copy(sum_c_all.at[me], sum_c_all.at[it], ca_ss.at[k], ca_rs.at[it], dev)
        return send, recv

    def far(t):
        by = 4 - lax.div(t + 1, 2)
        return wrap(jnp.where(lax.rem(t, 2) == 1, by, -by))

    def weights_of(t):
        g = far(t)
        s = scores[rows(g, GROUP), :]
        cl = col_wide[rows(g, GROUP), :]
        w = jnp.exp2(s - row_wide[...]) + jnp.exp2(s - jnp.concatenate([cl] * 4, axis=1))
        weights[rows(g, GROUP), :] = (w - jnp.where(mask_of(g), 1.0, 0.0)).astype(BF16)

    def tile(t, _):
        weights_of(t)
        return 0

    def q_copy(st, other):
        dev = (b, other)
        i, mine_i = st * NO + other, st * NO + o
        send = copy(q_out.at[i], q_in.at[mine_i], q_ss.at[i], q_rs.at[mine_i], dev)
        recv = copy(q_out.at[i], q_in.at[i], q_ss.at[i], q_rs.at[i], dev)
        return send, recv

    def q_stage(st):
        g = dot(weights[:, st * 256 : (st + 1) * 256], pall[...], TN)
        pres[...] = g

        def q_send(k, _):
            other, _dev = outer_peer(k)
            q_out[st * NO + other] = pres[rows(other, HALF), :].astype(BF16)
            q_copy(st, other)[0].start()
            return 0

        lax.fori_loop(1, NO, q_send, 0)
        q_own[st] = pres[rows(o, HALF), :]

    def sib_copy(i):
        return copy(sib_out.at[i], sib_in.at[i], sib_ss.at[i], sib_rs.at[i], sib)

    def slot(way, d, xx):
        return way * 8 + (d - 1) * 2 + xx

    def ring_copy(way, d, xx, h):
        i = slot(way, d, xx)
        part = pl.ds(h * HALF, HALF)
        return copy(
            ring_out.at[i, part], ring_in.at[i, part],
            ring_ss.at[i * 2 + h], ring_rs.at[i * 2 + h], up if way == 0 else down,
        )

    def arrived(way, d, xx, h):
        ring_copy(way, d, xx, h).wait_recv()
        return ring_in[slot(way, d, xx), h * HALF : (h + 1) * HALF, :].astype(F32)

    def joined(dz, xx, h):
        i = wrap(dz) * 2 + xx
        if h == 0:
            sib_copy(i).wait_recv()
        part = slice(h * HALF, (h + 1) * HALF)
        return mine[i, part, :] + sib_in[i, part, :].astype(F32)

    def ring_send(d, xx_up, carry):
        for h in range(2):
            for way, xx in ((0, xx_up), (1, 1 - xx_up)):
                value = joined(d if way == 0 else -d, xx, h)
                if carry:
                    value = value + arrived(way, d + 1, xx, h)
                ring_out[slot(way, d, xx), h * HALF : (h + 1) * HALF, :] = value.astype(BF16)
                ring_copy(way, d, xx, h).start()

    def last_copy(way, rel, h):
        i = slot(way, 1, rel)
        part = pl.ds(h * HALF, HALF)
        to = at(wrap(1 if way == 0 else -1), xh if rel == 0 else 1 - xh, c)
        return copy(
            ring_out.at[i, part], ring_in.at[i, part],
            ring_ss.at[i * 2 + h], ring_rs.at[i * 2 + h], to,
        )

    def last_send(rel):
        xx = xh if rel == 0 else 1 - xh
        for h in range(2):
            part = slice(h * HALF, (h + 1) * HALF)
            for way in range(2):
                value = joined(1 if way == 0 else -1, xx, h) + arrived(way, 2, xx, h)
                ring_out[slot(way, 1, rel), part, :] = value.astype(BF16)
                last_copy(way, rel, h).start()

    def x_copy(h):
        part = pl.ds(h * HALF, HALF)
        return copy(x_out.at[part], x_in.at[part], x_ss.at[h], x_rs.at[h], x2)

    def second(t, _):
        pl.when(t < 2)(lambda: weights_of(t))

        @pl.when(t == 2)
        def _():
            lax.fori_loop(2, NZ, tile, 0)
            q_stage(0)

        zz = far(t)
        pres[...] = SHARP * dot(weights[rows(zz, GROUP), :], qh[...], NN)
        for xx in range(2):
            i = zz * 2 + xx
            sib_out[i] = pres[rows(xx * 2 + 1 - c), :].astype(BF16)
            sib_copy(i).start()
            mine[i] = pres[rows(xx * 2 + c), :]
        pl.when(t == 1)(lambda: ring_send(4, 0, False))
        pl.when(t == 3)(lambda: ring_send(3, 1, False))
        return 0

    lax.fori_loop(0, 8, second, 0)
    q_stage(1)
    ring_send(3, 0, True)
    for h in range(2):
        x_out[h * HALF : (h + 1) * HALF, :] = joined(0, 1 - xh, h).astype(BF16)
        x_copy(h).start()

    def c_start(k, _):
        c_copy(k)[0].start()
        return 0

    lax.fori_loop(1, NO, c_start, 0)
    sib_r.wait_recv()
    sum_r_all[chip] = sum_r[...] + sum_r_sib[...]

    def r_copy(k):
        other, dev = chip_peer(k)
        send = copy(sum_r_all.at[chip], sum_r_all.at[chip], ra_ss.at[k], ra_rs.at[chip], dev)
        recv = copy(sum_r_all.at[chip], sum_r_all.at[other], ra_ss.at[k], ra_rs.at[other], dev)
        return send, recv

    def r_start(k, _):
        r_copy(k)[0].start()
        return 0

    lax.fori_loop(1, 16, r_start, 0)

    def ag_done(k, _):
        ag_copy(b, 0, k, sib).wait_send()
        return 0

    def as_done(k, _):
        as_copy(b, k).wait_send()
        return 0

    def row_done(k, _):
        row_copy(k)[0].wait_send()
        return 0

    def col_done(k, _):
        col_copy(k)[0].wait_send()
        return 0

    lax.fori_loop(0, sent[0], ag_done, 0)
    lax.fori_loop(0, sent[1], as_done, 0)
    lax.fori_loop(1, NO, row_done, 0)
    lax.fori_loop(1, 16, col_done, 0)
    sib_col.wait_send()
    sib_r.wait_send()
    ring_send(2, 1, True)
    ring_send(2, 0, True)

    def sib_done(k, _):
        sib_copy(k).wait_send()
        return 0

    lax.fori_loop(0, 16, sib_done, 0)

    def q_rows(st, other):
        return pl.ds(pl.multiple_of(st * 256 + other * HALF, HALF), HALF)

    def f_copy(st, k):
        other, dev = outer_peer(k)
        here, there = q_fin.at[q_rows(st, o)], q_fin.at[q_rows(st, other)]
        send = copy(q_done_rows.at[st], here, f_ss.at[st * NO + k], f_rs.at[st * NO + o], dev)
        recv = copy(q_done_rows.at[st], there, f_ss.at[st * NO + k], f_rs.at[st * NO + other], dev)
        return send, recv

    def f_own(st):
        return pltpu.make_async_copy(q_done_rows.at[st], q_fin.at[q_rows(st, o)], own_sem.at[st])

    def q_finish(st):
        def q_add(k, _):
            other, _dev = outer_peer(k)
            q_copy(st, other)[1].wait_recv()
            q_own[st] += q_in[st * NO + other].astype(F32)
            return 0

        lax.fori_loop(1, NO, q_add, 0)
        qv = q_ref[q_rows(st, o), :]
        q_inv = lax.rsqrt(jnp.sum(qv * qv, axis=1, keepdims=True) + EPS)
        qu = qv * q_inv
        qg = SHARP * q_own[st]
        q_done_rows[st] = (
            q_inv * (qg - qu * jnp.sum(qu * qg, axis=1, keepdims=True))
        ).astype(BF16)

        def f_start(k, _):
            f_copy(st, k)[0].start()
            return 0

        lax.fori_loop(1, NO, f_start, 0)
        f_own(st).start()

    q_finish(0)
    last_send(1)
    last_send(0)
    for way in range(2):
        for d, xx in ((4, way), (3, 0), (3, 1)):
            for h in range(2):
                ring_copy(way, d, xx, h).wait_send()
    q_finish(1)

    def q_done(k, _):
        for st in range(2):
            q_copy(st, outer_peer(k)[0])[0].wait_send()
        return 0

    lax.fori_loop(1, NO, q_done, 0)

    own_i = z * 2 + xh

    def last_arrived(way, rel, h):
        last_copy(way, rel, h).wait_recv()
        return ring_in[slot(way, 1, rel), h * HALF : (h + 1) * HALF, :].astype(F32)

    def c_wait(k, _):
        c_copy(k)[1].wait_recv()
        return 0

    def r_wait(k, _):
        r_copy(k)[1].wait_recv()
        return 0

    lax.fori_loop(1, NO, c_wait, 0)
    lax.fori_loop(1, 16, r_wait, 0)
    loss_ref[...] = (jnp.sum(sum_r_all[...], axis=0) + jnp.sum(sum_c_all[...], axis=0)) * (
        LN2 / (2.0 * NB * NP * NO)
    )

    pu = p_ref[...]
    p_inv2 = lax.rsqrt(jnp.sum(pu * pu, axis=1, keepdims=True) + EPS)
    pu = pu * p_inv2

    for h in range(2):
        part = slice(h * HALF, (h + 1) * HALF)
        x_copy(h).wait_recv()
        g = joined(0, xh, h) + x_in[part, :].astype(F32)
        for rel in (1, 0):
            g = g + last_arrived(0, rel, h) + last_arrived(1, rel, h)
        u = pu[part, :]
        po_ref[part, :] = p_inv2[part, :] * (g - u * jnp.sum(u * g, axis=1, keepdims=True))

    def f_wait(k, _):
        f_copy(0, k)[1].wait_recv()
        f_copy(1, k)[1].wait_recv()
        return 0

    lax.fori_loop(1, NO, f_wait, 0)

    for h in range(2):
        x_copy(h).wait_send()

    def outer_done(k, _):
        c_copy(k)[0].wait_send()
        for st in range(2):
            f_copy(st, k)[0].wait_send()
        return 0

    lax.fori_loop(1, NO, outer_done, 0)

    def chip_done(k, _):
        r_copy(k)[0].wait_send()
        return 0

    lax.fori_loop(1, 16, chip_done, 0)
    for way in range(2):
        for d in (1, 2):
            for xx in range(2):
                for h in range(2):
                    ring_copy(way, d, xx, h).wait_send()
    for st in range(2):
        f_own(st).wait()


def widen(q_ref, p_ref, loss_ref, qo_ref, po_ref, lo_ref):
    qo_ref[...] = q_ref[...].astype(F32)
    po_ref[...] = p_ref[...]
    lo_ref[...] = loss_ref[0:1, 0:1]


def per_device(queries, passages, positive_id):
    vmem = pl.BlockSpec(memory_space=pltpu.VMEM)
    hbm = pl.BlockSpec(memory_space=pl.ANY)
    dma = pltpu.SemaphoreType.DMA
    scratch = [
        pltpu.VMEM((NQ, D), F32),
        pltpu.VMEM((NP, D), F32),
        pltpu.VMEM((1, NQ), jnp.int32),
        dma((3,)),
        pltpu.VMEM((NB * NP, D), BF16),
        pltpu.VMEM((NQ, D), BF16),
        pltpu.VMEM((NB * NP, NQ), F32),
        pltpu.VMEM((NB * NP, NQ), BF16),
        pltpu.VMEM((16, NP, D), F32),
        pltpu.VMEM((GROUP, D), F32),
        pltpu.VMEM((16, NP, D), BF16),
        pltpu.VMEM((16, NP, D), BF16),
        pltpu.VMEM((16, NP, D), BF16),
        pltpu.VMEM((16, NP, D), BF16),
        pltpu.VMEM((NP, D), BF16),
        pltpu.VMEM((NP, D), BF16),
        pltpu.VMEM((2 * NO, HALF, D), BF16),
        pltpu.VMEM((2 * NO, HALF, D), BF16),
        pltpu.VMEM((2, HALF, D), F32),
        pltpu.VMEM((2, HALF, D), BF16),
        dma((2,)),
        pltpu.VMEM((8, NQ), F32),
        pltpu.VMEM((1, NQ), F32),
        pltpu.VMEM((1, NQ), F32),
        pltpu.VMEM((NZ, GROUP), F32),
        pltpu.VMEM((NZ, GROUP), F32),
        pltpu.VMEM((NB * NP, 128), F32),
        pltpu.VMEM((16, NZ, GROUP), F32),
        pltpu.VMEM((NO, 8, 128), F32),
        pltpu.VMEM((8, 128), F32),
        pltpu.VMEM((8, 128), F32),
        pltpu.VMEM((16, 8, 128), F32),
        pltpu.VMEM((NO, 8, 128), F32),
        dma((64,)), dma((2 * NB,)), dma((16,)),
        dma((1,)), dma((1,)),
        dma((16,)), dma((16,)),
        dma((NO,)), dma((NO,)),
        dma((16,)), dma((16,)),
        dma((32,)), dma((32,)),
        dma((2,)), dma((2,)),
        dma((2 * NO,)), dma((2 * NO,)),
        dma((2 * NO,)), dma((2 * NO,)),
        dma((1,)), dma((1,)),
        dma((16,)), dma((16,)),
        dma((NO,)), dma((NO,)),
    ]
    qd, pd, loss = pl.pallas_call(
        kernel,
        out_shape=(
            jax.ShapeDtypeStruct((NQ, D), BF16),
            jax.ShapeDtypeStruct((NP, D), F32),
            jax.ShapeDtypeStruct((8, 128), F32),
        ),
        in_specs=[hbm, hbm, hbm],
        out_specs=(hbm, vmem, vmem),
        scratch_shapes=scratch,
        compiler_params=pltpu.CompilerParams(
            collective_id=0, has_side_effects=True, vmem_limit_bytes=56 * 2**20
        ),
    )(queries, passages, positive_id.reshape(1, NQ))
    parts = 2
    return pl.pallas_call(
        widen,
        grid=(parts,),
        out_shape=(
            jax.ShapeDtypeStruct((NQ, D), F32),
            jax.ShapeDtypeStruct((NP, D), F32),
            jax.ShapeDtypeStruct((1, 1), F32),
        ),
        in_specs=[
            pl.BlockSpec((NQ // parts, D), lambda i: (i, 0)),
            pl.BlockSpec((NP // parts, D), lambda i: (i, 0)),
            pl.BlockSpec((8, 128), lambda i: (0, 0)),
        ],
        out_specs=(
            pl.BlockSpec((NQ // parts, D), lambda i: (i, 0)),
            pl.BlockSpec((NP // parts, D), lambda i: (i, 0)),
            pl.BlockSpec((1, 1), lambda i: (0, 0)),
        ),
    )(qd, pd, loss)


def solution(mesh):
    def step(queries, passages, positive_id):
        qd, pd, loss = per_device(queries, passages, positive_id)
        return qd, pd, loss.reshape(())

    placed = (P("blk", None), P(("outer", "blk"), None), P("blk"))
    return jax.shard_map(
        step,
        mesh=mesh,
        in_specs=placed,
        out_specs=(P("blk", None), P(("outer", "blk"), None), P()),
        check_vma=False,
    )
```
